256 devices in a mesh: pos: 32 (over x, z), head: 8 (over y, core).
Axes of the slice: x: 4, y: 4, z: 8, core: 2. Of those that a mesh axis runs over, the one named last changes fastest.
Arguments:
- query: bfloat16 [8192, 12288], P('pos', 'head'), may hold values from -8 to 8
- latent: bfloat16 [8192, 576], P('pos'), may hold values from -8 to 8
- norm_gain: float32 [512], replicated, may hold values from 0.25 to 1.75
- key_up: bfloat16 [512, 64, 128], P(None, 'head'), may hold values from -0.25 to 0.25
- value_up: bfloat16 [512, 64, 128], P(None, 'head'), may hold values from -0.25 to 0.25
- out_grad: bfloat16 [8192, 8192], P('pos', 'head'), may hold values from -6 to 6
- ancestors: int32 [64, 4], P('pos'), may hold values from 0 to 63, as said below
- visible: int32 [64, 4], P('pos'), may hold values from 1 to 128
Outputs:
- attn_out: bfloat16 [8192, 8192], P('pos', 'head')
- query_grad: bfloat16 [8192, 12288], P('pos', 'head')
- latent_grad: float32 [8192, 576], P('pos')
- key_up_grad: float32 [512, 64, 128], P('pos', 'head')
- value_up_grad: float32 [512, 64, 128], P('pos', 'head')
The draws below stay inside these ranges and needn't reach their ends.
Inputs may be any that keep to these rules, and one draw needn't show every extreme that they name: `ancestors`: blocks are numbered globally, 2 consecutive ones to each index of pos. In one row the listed blocks are distinct and differ from the row's own block. Blocks held by pos index 0 may be listed by any row; for every pos index d and every other pos index s of 1 or more, all rows held by d name at most one block of s.
All inputs are finite; a program needn't handle non-finite values.
Results may differ from the reference program's by a relative error of at most 0.02.
Values may be sent and summed in bfloat16 or wider, within the bound.
No kernel may reach another device: no remote copies, remote signals or barrier semaphores. Data moves between devices by JAX's collectives and lax.ppermute only.
A program may use at most 128 MiB of HBM per device.

```python
import math
import jax
import jax.numpy as jnp
from jax import lax

LATENT = 512
ROPE = 64
HEAD_DIM = 128
HEADS = 64
BLOCK = 128
SLOTS = 4
TOKENS = 8192
BLOCKS_DEV = 2
NBLK = 64
N_POS = 32


def tree_lists(base_key):
    streams = jax.random.split(base_key, 8)
    blocks = jnp.arange(NBLK, dtype=jnp.int32)
    device = blocks // BLOCKS_DEV
    within = blocks % BLOCKS_DEV
    sources = jnp.arange(N_POS, dtype=jnp.int32)
    slot_numbers = jnp.arange(SLOTS, dtype=jnp.int32)
    pick_total = min(BLOCKS_DEV * SLOTS - 1, N_POS - 2)
    source_block = jax.random.randint(streams[0], (N_POS, N_POS), 0, BLOCKS_DEV)
    lottery = jax.random.randint(streams[1], (N_POS, N_POS), 0, 1 << 20) * N_POS + sources[None, :]
    usable = (sources[None, :] >= 1) & (sources[None, :] != sources[:, None])
    ranked = jnp.where(usable, lottery, -1 - sources[None, :])
    top_scores, picked = lax.top_k(ranked, pick_total)
    flat = within[:, None] * SLOTS + slot_numbers[None, :] - 1
    pick_at = jnp.mod(flat, pick_total).astype(jnp.int32)
    remote_src = jnp.take_along_axis(picked[device], pick_at, axis=1)
    remote_ids = remote_src * BLOCKS_DEV + jnp.take_along_axis(source_block[device], remote_src, axis=1)
    partial_seen = jax.random.randint(streams[2], (NBLK, SLOTS), 1, BLOCK + 1)
    whole_block = jax.random.randint(streams[3], (NBLK, SLOTS), 0, 2) == 0
    remote_seen = jnp.where(whole_block, BLOCK, partial_seen)
    other_pick = jax.random.randint(streams[4], (NBLK,), 0, BLOCKS_DEV)
    self_pick = jax.random.randint(streams[5], (NBLK,), 0, BLOCKS_DEV - 1)
    trunk_block = jnp.where(device == 0, jnp.mod(within + 1 + self_pick, BLOCKS_DEV), other_pick)
    trunk_edge = jax.random.randint(streams[6], (NBLK,), 1, BLOCK + 1)
    is_trunk = flat == -1
    listed = jnp.where(is_trunk, trunk_block[:, None], remote_ids)
    seen_len = jnp.where(is_trunk, trunk_edge[:, None], remote_seen)
    shuffle = jax.random.randint(streams[7], (NBLK, SLOTS), 0, 1 << 20) * SLOTS + slot_numbers[None, :]
    slot_order = jnp.argsort(shuffle, axis=1)
    return (jnp.take_along_axis(listed, slot_order, axis=1).astype(jnp.int32), jnp.take_along_axis(seen_len, slot_order, axis=1).astype(jnp.int32))


def draw_ancestors(key, part):
    listed, seen_len = tree_lists(key)
    return listed


def draw_visible(key, part):
    listed, seen_len = tree_lists(key)
    return seen_len


def draw_query(key, part):
    key = jax.random.fold_in(key, 13)
    values = jnp.clip(jax.random.normal(key, (TOKENS, HEADS, HEAD_DIM + ROPE), jnp.float32), -8.0, 8.0)
    return values.reshape(TOKENS, HEADS * (HEAD_DIM + ROPE)).astype(jnp.bfloat16)


def draw_latent(key, part):
    key = jax.random.fold_in(key, 11)
    values = jnp.clip(jax.random.normal(key, (TOKENS, LATENT + ROPE), jnp.float32), -8.0, 8.0)
    return values.astype(jnp.bfloat16)


def block_levels(own_key, shape, shards, least, largest):
    loudness, own = 1.0, jax.random.fold_in(own_key, 6)
    for axis_at, parts in shards:
        heights = jnp.exp(jax.random.uniform(jax.random.fold_in(own, axis_at), (parts,), jnp.float32, least / len(shards), largest / len(shards)))
        loudness = loudness * jnp.repeat(heights, shape[axis_at] // parts).reshape([-1 if axis == axis_at else 1 for axis in range(len(shape))])
    return loudness


def scatter_about(rng, dims, width, most, cuts=(), held_as=jnp.bfloat16):
    values = jax.random.normal(rng, dims, jnp.float32) * width
    if len(cuts) > 0:
        values = block_levels(rng, dims, cuts, -0.22, 0.18) * values
    return jnp.clip(values, min=-most, max=most).astype(held_as)


def setup_inputs(seed: int = 0) -> dict:
    key_list = jax.random.split(jax.random.key(seed), 9)
    return {
        "query": draw_query(jax.random.fold_in(key_list[8], 71), 0),
        "latent": draw_latent(jax.random.fold_in(key_list[8], 71), 0),
        "norm_gain": jnp.clip(1.0 + 0.15 * jax.random.normal(key_list[2], (LATENT,), jnp.float32), 0.25, 1.75),
        "key_up": scatter_about(key_list[3], (LATENT, HEADS, HEAD_DIM), LATENT ** -0.5, 0.25, ((1, 8),)),
        "value_up": scatter_about(key_list[4], (LATENT, HEADS, HEAD_DIM), LATENT ** -0.5, 0.25, ((1, 8),)),
        "out_grad": scatter_about(key_list[5], (TOKENS, HEADS * HEAD_DIM), 1.0, 6.0, ((0, 32), (1, 8))),
        "ancestors": draw_ancestors(jax.random.fold_in(key_list[8], 71), 0),
        "visible": draw_visible(jax.random.fold_in(key_list[8], 71), 0),
    }


norm_epsilon = 1e-06

def rounded(values):
    return lax.optimization_barrier(values.astype(jnp.bfloat16))

def reference(query, latent, norm_gain, key_up, value_up, out_grad, ancestors, visible):
    kv_width = LATENT + ROPE
    tokens = latent.shape[0]
    block_total = tokens // BLOCK
    score_scale = 1.0 / math.sqrt(HEAD_DIM + ROPE)
    latent_raw = latent[:, :LATENT].astype(jnp.float32)
    inverse = lax.rsqrt(lax.optimization_barrier(jnp.mean(latent_raw * latent_raw, axis=1, keepdims=True)) + norm_epsilon)
    normed = rounded(latent_raw * inverse * norm_gain)
    key_rows = jnp.concatenate([normed, latent[:, LATENT:]], axis=1)
    all_tiles = key_rows.reshape(block_total, BLOCK, kv_width)
    key_up_f = key_up.astype(jnp.float32)
    value_up_f = value_up.astype(jnp.float32)
    query_heads = query.reshape(tokens, HEADS, HEAD_DIM + ROPE)
    query_nope = query_heads[:, :, :HEAD_DIM].astype(jnp.float32)
    absorbed = rounded(jnp.einsum('thd,lhd->thl', query_nope, key_up_f))
    query_full = jnp.concatenate([absorbed, query_heads[:, :, HEAD_DIM:]], axis=2).reshape(block_total, BLOCK, HEADS, kv_width)
    grad_heads = out_grad.reshape(block_total, BLOCK, HEADS, HEAD_DIM)
    tile_ids = jnp.concatenate([jnp.arange(block_total, dtype=jnp.int32)[:, None], ancestors.astype(jnp.int32)], axis=1)
    offsets = jnp.arange(BLOCK, dtype=jnp.int32)
    causal = offsets[None, :] <= offsets[:, None]

    def one_block(inputs):
        query_block, grad_block, listed, limits = inputs
        tiles = all_tiles[listed].reshape((SLOTS + 1) * BLOCK, kv_width).astype(jnp.float32)
        seen_slots = offsets[None, :] < limits[:, None]
        allowed = jnp.concatenate([causal[:, None, :], jnp.broadcast_to(seen_slots[None], (BLOCK, SLOTS, BLOCK))], axis=1).reshape(BLOCK, (SLOTS + 1) * BLOCK)
        query_f = query_block.astype(jnp.float32)
        scores = jnp.einsum('qhx,kx->qhk', query_f, tiles) * score_scale
        scores = jnp.where(allowed[:, None, :], scores, -jnp.inf)
        exp_terms = jnp.exp(scores - lax.optimization_barrier(jnp.max(scores, axis=2, keepdims=True)))
        weights = exp_terms / lax.optimization_barrier(jnp.sum(exp_terms, axis=2, keepdims=True))
        weights_half = rounded(weights).astype(jnp.float32)
        mixed = rounded(jnp.einsum('qhk,kl->qhl', weights_half, tiles[:, :LATENT]))
        attention = jnp.einsum('qhl,lhd->qhd', mixed.astype(jnp.float32), value_up_f).astype(jnp.bfloat16)
        mixed_grad = rounded(jnp.einsum('qhd,lhd->qhl', grad_block.astype(jnp.float32), value_up_f)).astype(jnp.float32)
        weight_grad = jnp.einsum('qhl,kl->qhk', mixed_grad, tiles[:, :LATENT])
        score_grad = rounded(weights * (weight_grad - lax.optimization_barrier(jnp.sum(weights * weight_grad, axis=2, keepdims=True))) * score_scale).astype(jnp.float32)
        full_grad = jnp.einsum('qhk,kx->qhx', score_grad, tiles)
        tile_grad = jnp.einsum('qhk,qhx->kx', score_grad, query_f)
        value_part = jnp.einsum('qhk,qhl->kl', weights_half, mixed_grad)
        tile_grad = tile_grad + jnp.pad(value_part, ((0, 0), (0, ROPE)))
        return (attention, mixed, full_grad, tile_grad.reshape(SLOTS + 1, BLOCK, kv_width))
    attention, mixed, full_grad, tile_grads = lax.map(one_block, (query_full, grad_heads, tile_ids, visible.astype(jnp.int32)))
    absorbed_grad = rounded(full_grad[..., :LATENT]).astype(jnp.float32).reshape(tokens, HEADS, LATENT)
    nope_grad = jnp.einsum('thl,lhd->thd', absorbed_grad, key_up_f)
    query_grad = jnp.concatenate([nope_grad, full_grad[..., LATENT:].reshape(tokens, HEADS, ROPE)], axis=2).astype(jnp.bfloat16).reshape(tokens, HEADS * (HEAD_DIM + ROPE))
    key_up_grad = jnp.einsum('thl,thd->lhd', absorbed_grad, query_nope)
    value_up_grad = jnp.einsum('thl,thd->lhd', mixed.astype(jnp.float32).reshape(tokens, HEADS, LATENT), grad_heads.astype(jnp.float32).reshape(tokens, HEADS, HEAD_DIM))
    keys_grad = jnp.zeros((block_total, BLOCK, kv_width), jnp.float32).at[tile_ids.reshape(-1)].add(tile_grads.reshape(-1, BLOCK, kv_width)).reshape(tokens, kv_width)
    gained = keys_grad[:, :LATENT] * norm_gain
    latent_part = inverse * gained - latent_raw * inverse * inverse * inverse * lax.optimization_barrier(jnp.mean(latent_raw * gained, axis=1, keepdims=True))
    latent_grad = jnp.concatenate([latent_part, keys_grad[:, LATENT:]], axis=1)
    return (attention.reshape(tokens, HEADS * HEAD_DIM), query_grad, latent_grad, key_up_grad, value_up_grad)
```

```python
import functools
import math

import jax
import jax.numpy as jnp
from jax import lax
from jax.experimental import pallas as pl
from jax.experimental.pallas import tpu as pltpu
from jax.sharding import Mesh
from jax.sharding import PartitionSpec as P

LATENT = 512
ROPE = 64
KV = LATENT + ROPE
HEAD_DIM = 128
QDIM = HEAD_DIM + ROPE
BLOCK = 128
SLOTS = 4
BLOCKS_DEV = 2
NX, NZ, NY, NC = 4, 8, 4, 2
SHARES = NY * NC
ROWS = BLOCK // SHARES
HALF = NY * ROWS
HEADS_DEV = 8
TILES = BLOCKS_DEV * (1 + SLOTS)
KEYS = (1 + SLOTS) * BLOCK
HEADS_STEP = 2
norm_epsilon = 1e-06

bf16 = jnp.bfloat16
f32 = jnp.float32
VMEM_LIMIT = 48 * 1024 * 1024


def dot(a, b):
    return lax.dot_general(a, b, (((1,), (0,)), ((), ())), preferred_element_type=f32)


def dot_nt(a, b):
    return lax.dot_general(a, b, (((1,), (1,)), ((), ())), preferred_element_type=f32)


def dot_tn(a, b):
    return lax.dot_general(a, b, (((0,), (0,)), ((), ())), preferred_element_type=f32)


def smem():
    return pl.BlockSpec(memory_space=pltpu.SMEM)


def vmem():
    return pl.BlockSpec(memory_space=pltpu.VMEM)


def norm_inverse(raw):
    return lax.rsqrt(jnp.mean(raw * raw, axis=1, keepdims=True) + norm_epsilon)


def share_kernel(share_ref, latent_ref, gain_ref, out_ref):
    for b in range(BLOCKS_DEV):
        start = pl.multiple_of(b * BLOCK + share_ref[0] * ROWS, ROWS)
        raw = latent_ref[pl.ds(start, ROWS), :LATENT].astype(f32)
        keys = (raw * norm_inverse(raw) * gain_ref[...]).astype(bf16)
        rope = latent_ref[pl.ds(start, ROWS), LATENT:]
        for z in range(NZ):
            out_ref[z, b, :, :LATENT] = keys
            out_ref[z, b, :, LATENT:] = rope


def spread_kernel(in_ref, out_ref):
    for x in range(NX):
        out_ref[x] = in_ref[...]


def select_kernel(anc_ref, all_ref, out_ref):
    for s in range(BLOCKS_DEV * SLOTS):
        tile = all_ref[anc_ref[s]]
        for y in range(NY):
            out_ref[y, s] = tile


def attend_kernel(
    core_ref, vis_ref, query_ref, grad_ref, key_up_ref, value_up_ref, latent_ref, gain_ref, near_ref, far_ref,
    attn_ref, qgrad_ref, wgrad_ref, keep_ref, send_ref,
    klat, krope, bias, glat, grope,
):
    step = pl.program_id(0)
    core = core_ref[0]
    scale = 1.0 / math.sqrt(QDIM)

    @pl.when(step == 0)
    def _():
        raw = latent_ref[:, :LATENT].astype(f32)
        own = (raw * norm_inverse(raw) * gain_ref[...]).astype(bf16)
        own = own.reshape(BLOCKS_DEV, NY, NC, ROWS, LATENT)
        rope = latent_ref[:, LATENT:].reshape(BLOCKS_DEV, NY, NC, ROWS, ROPE)
        for b in range(BLOCKS_DEV):
            for side in range(NC):
                for y in range(NY):
                    at = side * HALF + y * ROWS
                    first = core == side
                    klat[b, at : at + ROWS, :] = jnp.where(first, own[b, y, 0], own[b, y, 1])
                    krope[b, at : at + ROWS, :] = jnp.where(first, rope[b, y, 0], rope[b, y, 1])
                    for j in range(SLOTS):
                        src = (near_ref, far_ref)[side]
                        to = (1 + j) * BLOCK + at
                        klat[b, to : to + ROWS, :] = src[y, b * SLOTS + j, :, :LATENT]
                        krope[b, to : to + ROWS, :] = src[y, b * SLOTS + j, :, LATENT:]
        col = lax.broadcasted_iota(jnp.int32, (BLOCK, BLOCK), 1)
        row = lax.broadcasted_iota(jnp.int32, (BLOCK, BLOCK), 0)
        side = jnp.where(col >= HALF, 1, 0)
        rest = col - side * HALF
        piece = rest // ROWS
        owner = jnp.where(core == 0, side, 1 - side)
        offset = (piece * NC + owner) * ROWS + (rest - piece * ROWS)
        for b in range(BLOCKS_DEV):
            bias[b, :, :BLOCK] = jnp.where(offset <= row, 0.0, -jnp.inf)
            for j in range(SLOTS):
                limit = vis_ref[b * SLOTS + j]
                bias[b, :, (1 + j) * BLOCK : (2 + j) * BLOCK] = jnp.where(offset < limit, 0.0, -jnp.inf)
        glat[...] = jnp.zeros_like(glat)
        grope[...] = jnp.zeros_like(grope)

    heads = range(HEADS_STEP)
    nope = [query_ref[:, h * QDIM : h * QDIM + HEAD_DIM] for h in heads]
    rope = [query_ref[:, h * QDIM + HEAD_DIM : (h + 1) * QDIM] for h in heads]
    grad = [grad_ref[:, h * HEAD_DIM : (h + 1) * HEAD_DIM] for h in heads]
    key_up = [key_up_ref[:, h * HEAD_DIM : (h + 1) * HEAD_DIM] for h in heads]
    value_up = [value_up_ref[:, h * HEAD_DIM : (h + 1) * HEAD_DIM] for h in heads]
    absorbed = [dot_nt(nope[h], key_up[h]).astype(bf16) for h in heads]
    mixed_grad = [dot_nt(grad[h], value_up[h]).astype(bf16) for h in heads]

    mixed_parts, full_parts, rope_parts = [], [], []
    for b in range(BLOCKS_DEV):
        rows = slice(b * BLOCK, (b + 1) * BLOCK)
        ab = jnp.concatenate([absorbed[h][rows] for h in heads], axis=0)
        rb = jnp.concatenate([rope[h][rows] for h in heads], axis=0)
        mg = jnp.concatenate([mixed_grad[h][rows] for h in heads], axis=0)
        lat = klat[b]
        rop = krope[b]
        mask = jnp.concatenate([bias[b]] * HEADS_STEP, axis=0)
        scores = (dot_nt(ab, lat) + dot_nt(rb, rop)) * scale + mask
        exp_terms = jnp.exp(scores - jnp.max(scores, axis=1, keepdims=True))
        weights = exp_terms * (1.0 / jnp.sum(exp_terms, axis=1, keepdims=True))
        half = weights.astype(bf16)
        mixed_parts.append(dot(half, lat).astype(bf16))
        weight_grad = dot_nt(mg, lat)
        inner = jnp.sum(weights * weight_grad, axis=1, keepdims=True)
        score_grad = (weights * (weight_grad - inner) * scale).astype(bf16)
        full_parts.append(dot(score_grad, lat).astype(bf16))
        rope_parts.append(dot(score_grad, rop).astype(bf16))
        both = jnp.concatenate([score_grad, half], axis=0)
        glat[b] += dot_tn(both, jnp.concatenate([ab, mg], axis=0))
        grope[b] += dot_tn(score_grad, rb)

    def head_rows(parts, h):
        return jnp.concatenate([part[h * BLOCK : (h + 1) * BLOCK] for part in parts], axis=0)

    width = HEADS_STEP * HEAD_DIM
    for h in heads:
        mixed = head_rows(mixed_parts, h)
        full = head_rows(full_parts, h)
        attn_ref[:, h * HEAD_DIM : (h + 1) * HEAD_DIM] = dot(mixed, value_up[h]).astype(bf16)
        qgrad_ref[:, h * QDIM : h * QDIM + HEAD_DIM] = dot(full, key_up[h]).astype(bf16)
        qgrad_ref[:, h * QDIM + HEAD_DIM : (h + 1) * QDIM] = head_rows(rope_parts, h)
        at = h * HEAD_DIM
        wgrad_ref[:, at : at + HEAD_DIM] = dot_tn(full, nope[h]).astype(bf16)
        wgrad_ref[:, width + at : width + at + HEAD_DIM] = dot_tn(mixed, grad[h]).astype(bf16)

    @pl.when(step == pl.num_programs(0) - 1)
    def _():
        for b in range(BLOCKS_DEV):
            for j in range(1 + SLOTS):
                tile = b if j == 0 else BLOCKS_DEV + b * SLOTS + j - 1
                for y in range(NY):
                    at = j * BLOCK + y * ROWS
                    keep_ref[y, tile, :, :LATENT] = glat[b, at : at + ROWS, :]
                    keep_ref[y, tile, :, LATENT:] = grope[b, at : at + ROWS, :]
                    at = at + HALF
                    send_ref[y, tile, :, :LATENT] = glat[b, at : at + ROWS, :].astype(bf16)
                    send_ref[y, tile, :, LATENT:] = grope[b, at : at + ROWS, :].astype(bf16)


def pair_kernel(keep_ref, recv_ref, out_ref):
    out_ref[...] = (keep_ref[...] + recv_ref[...].astype(f32)).astype(bf16)


def scatter_kernel(dest_ref, in_ref, out_ref, acc):
    acc[...] = jnp.zeros_like(acc)
    for t in range(TILES):
        tile = in_ref[0, t].astype(f32)
        for y in range(1, NY):
            tile = tile + in_ref[y, t].astype(f32)
        at = dest_ref[t]
        acc[at] = acc[at] + tile
    out_ref[...] = acc[...].astype(bf16)


def sum_kernel(in_ref, out_ref):
    total = in_ref[0].astype(f32)
    for i in range(1, in_ref.shape[0]):
        total = total + in_ref[i].astype(f32)
    total = total.astype(bf16)
    if len(out_ref.shape) == len(total.shape):
        out_ref[...] = total
    else:
        for i in range(out_ref.shape[0]):
            out_ref[i] = total


def final_kernel(core_ref, near_ref, far_ref, latent_ref, gain_ref, out_ref):
    core = core_ref[0]
    for b in range(BLOCKS_DEV):
        pieces = []
        for y in range(NY):
            near, far = near_ref[y, b], far_ref[y, b]
            pieces.append(jnp.where(core == 0, near, far))
            pieces.append(jnp.where(core == 0, far, near))
        total = jnp.concatenate(pieces, axis=0).astype(f32)
        rows = slice(b * BLOCK, (b + 1) * BLOCK)
        raw = latent_ref[rows, :LATENT].astype(f32)
        inverse = norm_inverse(raw)
        gained = total[:, :LATENT] * gain_ref[...]
        out_ref[rows, :LATENT] = inverse * gained - raw * inverse * inverse * inverse * jnp.mean(
            raw * gained, axis=1, keepdims=True
        )
        out_ref[rows, LATENT:] = total[:, LATENT:]


def call(kernel, out_shape, in_specs, **kw):
    return pl.pallas_call(
        kernel,
        out_shape=out_shape,
        in_specs=in_specs,
        out_specs=kw.pop("out_specs", vmem()),
        compiler_params=pltpu.CompilerParams(vmem_limit_bytes=VMEM_LIMIT),
        **kw,
    )


def shape(*dims, dtype=bf16):
    return jax.ShapeDtypeStruct(dims, dtype)


def exchange(values, axis):
    return lax.all_to_all(values, axis, split_axis=0, concat_axis=0, tiled=True)


def swap_cores(values):
    return lax.ppermute(values, "c", [(0, 1), (1, 0)])


def shards(query, latent, norm_gain, key_up, value_up, out_grad, ancestors, visible):
    core = lax.axis_index("c").astype(jnp.int32).reshape(1)
    share = (lax.axis_index("y") * NC + lax.axis_index("c")).astype(jnp.int32).reshape(1)
    place = lax.axis_index("x") * NZ + lax.axis_index("z")
    gain = norm_gain.reshape(1, LATENT)
    listed = ancestors.reshape(BLOCKS_DEV * SLOTS)
    limits = visible.reshape(BLOCKS_DEV * SLOTS)

    mine = call(share_kernel, shape(NZ, BLOCKS_DEV, ROWS, KV), [smem(), vmem(), vmem()])(share, latent, gain)
    column = exchange(mine, "z").reshape(NZ * BLOCKS_DEV, ROWS, KV)
    column = call(spread_kernel, shape(NX, NZ * BLOCKS_DEV, ROWS, KV), [vmem()])(column)
    everyone = exchange(column, "x").reshape(NX * NZ * BLOCKS_DEV, ROWS, KV)
    picked = call(select_kernel, shape(NY, BLOCKS_DEV * SLOTS, ROWS, KV), [smem(), vmem()])(listed, everyone)
    near = exchange(picked, "y")
    far = swap_cores(near)

    key_up_flat = key_up.reshape(LATENT, HEADS_DEV * HEAD_DIM)
    value_up_flat = value_up.reshape(LATENT, HEADS_DEV * HEAD_DIM)
    tokens = query.shape[0]
    steps = HEADS_DEV // HEADS_STEP
    width = HEADS_STEP * HEAD_DIM
    qwidth = HEADS_STEP * QDIM

    def columns(rows, cols):
        return pl.BlockSpec((rows, cols), lambda g: (0, g))

    def whole(*dims):
        return pl.BlockSpec(dims, lambda g: (0,) * len(dims))

    attn_out, query_grad, wgrad, keep, send = call(
        attend_kernel,
        (
            shape(tokens, HEADS_DEV * HEAD_DIM),
            shape(tokens, HEADS_DEV * QDIM),
            shape(LATENT, 2 * HEADS_DEV * HEAD_DIM),
            shape(NY, TILES, ROWS, KV, dtype=f32),
            shape(NY, TILES, ROWS, KV),
        ),
        [
            smem(),
            smem(),
            columns(tokens, qwidth),
            columns(tokens, width),
            columns(LATENT, width),
            columns(LATENT, width),
            whole(tokens, KV),
            whole(1, LATENT),
            whole(NY, BLOCKS_DEV * SLOTS, ROWS, KV),
            whole(NY, BLOCKS_DEV * SLOTS, ROWS, KV),
        ],
        out_specs=(
            columns(tokens, width),
            columns(tokens, qwidth),
            columns(LATENT, 2 * width),
            whole(NY, TILES, ROWS, KV),
            whole(NY, TILES, ROWS, KV),
        ),
        grid=(steps,),
        scratch_shapes=[
            pltpu.VMEM((BLOCKS_DEV, KEYS, LATENT), bf16),
            pltpu.VMEM((BLOCKS_DEV, KEYS, ROPE), bf16),
            pltpu.VMEM((BLOCKS_DEV, BLOCK, KEYS), f32),
            pltpu.VMEM((BLOCKS_DEV, KEYS, LATENT), f32),
            pltpu.VMEM((BLOCKS_DEV, KEYS, ROPE), f32),
        ],
        cost_estimate=pl.CostEstimate(flops=11_000_000_000, bytes_accessed=16_000_000, transcendentals=1_400_000),
    )(core, limits, query, out_grad, key_up_flat, value_up_flat, latent, gain, near, far)

    wgrad = lax.psum_scatter(wgrad, "x", scatter_dimension=0, tiled=True)
    wgrad = lax.psum_scatter(wgrad, "z", scatter_dimension=0, tiled=True)
    wgrad = wgrad.astype(f32).reshape(LATENT // (NX * NZ), steps, 2, HEADS_STEP, HEAD_DIM)
    key_up_grad = wgrad[:, :, 0].reshape(-1, HEADS_DEV, HEAD_DIM)
    value_up_grad = wgrad[:, :, 1].reshape(-1, HEADS_DEV, HEAD_DIM)

    paired = call(pair_kernel, shape(NY, TILES, ROWS, KV), [vmem(), vmem()])(keep, swap_cores(send))
    paired = exchange(paired, "y")
    dest = jnp.concatenate([place * BLOCKS_DEV + jnp.arange(BLOCKS_DEV, dtype=jnp.int32), listed])
    spread = call(
        scatter_kernel,
        shape(NX * NZ * BLOCKS_DEV, ROWS, KV),
        [smem(), vmem()],
        scratch_shapes=[pltpu.VMEM((NX * NZ * BLOCKS_DEV, ROWS, KV), f32)],
    )(dest, paired)
    spread = exchange(spread.reshape(NX, NZ * BLOCKS_DEV, ROWS, KV), "x")
    line = call(sum_kernel, shape(NZ * BLOCKS_DEV, ROWS, KV), [vmem()])(spread)
    line = exchange(line.reshape(NZ, BLOCKS_DEV, ROWS, KV), "z")
    total = call(sum_kernel, shape(NY, BLOCKS_DEV, ROWS, KV), [vmem()])(line)
    total = exchange(total, "y")
    latent_grad = call(
        final_kernel, shape(tokens, KV, dtype=f32), [smem(), vmem(), vmem(), vmem(), vmem()]
    )(core, total, swap_cores(total), latent, gain)
    return attn_out, query_grad, latent_grad, key_up_grad, value_up_grad


def solution(mesh):
    grid = Mesh(mesh.devices.reshape(NX, NZ, NY, NC), ("x", "z", "y", "c"))
    pos, head = ("x", "z"), ("y", "c")
    return jax.shard_map(
        shards,
        mesh=grid,
        in_specs=(
            P(pos, head),
            P(pos, None),
            P(),
            P(None, head, None),
            P(None, head, None),
            P(pos, head),
            P(pos, None),
            P(pos, None),
        ),
        out_specs=(
            P(pos, head),
            P(pos, head),
            P(pos, None),
            P(pos, head, None),
            P(pos, head, None),
        ),
        check_vma=False,
    )
```

```python
import functools
import math

import jax
import jax.numpy as jnp
from jax import lax
from jax.experimental import pallas as pl
from jax.experimental.pallas import tpu as pltpu
from jax.sharding import Mesh
from jax.sharding import PartitionSpec as P

LATENT = 512
ROPE = 64
KV = LATENT + ROPE
HEAD_DIM = 128
QDIM = HEAD_DIM + ROPE
BLOCK = 128
SLOTS = 4
BLOCKS_DEV = 2
NX, NZ, NY, NC = 4, 8, 4, 2
SHARES = NY * NC
ROWS = BLOCK // SHARES
HALF = NY * ROWS
HEADS_DEV = 8
TILES = BLOCKS_DEV * (1 + SLOTS)
KEYS = (1 + SLOTS) * BLOCK
COLUMN = NZ * BLOCKS_DEV
PART = LATENT // NX
HEADS_STEP = 4
norm_epsilon = 1e-06

bf16 = jnp.bfloat16
f32 = jnp.float32
VMEM_LIMIT = 48 * 1024 * 1024


def dot(a, b):
    return lax.dot_general(a, b, (((1,), (0,)), ((), ())), preferred_element_type=f32)


def dot_nt(a, b):
    return lax.dot_general(a, b, (((1,), (1,)), ((), ())), preferred_element_type=f32)


def dot_tn(a, b):
    return lax.dot_general(a, b, (((0,), (0,)), ((), ())), preferred_element_type=f32)


def smem():
    return pl.BlockSpec(memory_space=pltpu.SMEM)


def vmem():
    return pl.BlockSpec(memory_space=pltpu.VMEM)


def norm_inverse(raw):
    return lax.rsqrt(jnp.mean(raw * raw, axis=1, keepdims=True) + norm_epsilon)


def share_kernel(share_ref, latent_ref, gain_ref, out_ref):
    for b in range(BLOCKS_DEV):
        start = pl.multiple_of(b * BLOCK + share_ref[0] * ROWS, ROWS)
        raw = latent_ref[pl.ds(start, ROWS), :LATENT].astype(f32)
        keys = (raw * norm_inverse(raw) * gain_ref[...]).astype(bf16)
        rope = latent_ref[pl.ds(start, ROWS), LATENT:]
        for z in range(NZ):
            out_ref[z, b, :, :LATENT] = keys
            out_ref[z, b, :, LATENT:] = rope


def spread_kernel(x_ref, l0, l1, l2, l3, column_ref, out_ref):
    for r, listed in enumerate((l0, l1, l2, l3)):
        to = (x_ref[0] + r) % NX
        for s in range(BLOCKS_DEV * SLOTS):
            out_ref[to, s] = column_ref[listed[s] % COLUMN]


def select_kernel(listed_ref, all_ref, out_ref):
    for s in range(BLOCKS_DEV * SLOTS):
        tile = all_ref[listed_ref[s] // COLUMN, s]
        for y in range(NY):
            out_ref[y, s] = tile


def attend_kernel(
    core_ref, vis_ref, query_ref, grad_ref, key_up_ref, value_up_ref, latent_ref, gain_ref, near_ref, far_ref,
    sgrad_ref, weights_ref, klat, krope, keep_ref, send_ref,
    bias, glat, grope,
):
    step = pl.program_id(0)
    core = core_ref[0]
    scale = 1.0 / math.sqrt(QDIM)

    @pl.when(step == 0)
    def _():
        raw = latent_ref[:, :LATENT].astype(f32)
        own = (raw * norm_inverse(raw) * gain_ref[...]).astype(bf16)
        own = own.reshape(BLOCKS_DEV, NY, NC, ROWS, LATENT)
        rope = latent_ref[:, LATENT:].reshape(BLOCKS_DEV, NY, NC, ROWS, ROPE)
        for b in range(BLOCKS_DEV):
            for side in range(NC):
                for y in range(NY):
                    at = side * HALF + y * ROWS
                    first = core == side
                    klat[b, at : at + ROWS, :] = jnp.where(first, own[b, y, 0], own[b, y, 1])
                    krope[b, at : at + ROWS, :] = jnp.where(first, rope[b, y, 0], rope[b, y, 1])
                    for j in range(SLOTS):
                        src = (near_ref, far_ref)[side]
                        to = (1 + j) * BLOCK + at
                        klat[b, to : to + ROWS, :] = src[y, b * SLOTS + j, :, :LATENT]
                        krope[b, to : to + ROWS, :] = src[y, b * SLOTS + j, :, LATENT:]
        col = lax.broadcasted_iota(jnp.int32, (BLOCK, BLOCK), 1)
        row = lax.broadcasted_iota(jnp.int32, (BLOCK, BLOCK), 0)
        side = jnp.where(col >= HALF, 1, 0)
        rest = col - side * HALF
        piece = rest // ROWS
        owner = jnp.where(core == 0, side, 1 - side)
        offset = (piece * NC + owner) * ROWS + (rest - piece * ROWS)
        for b in range(BLOCKS_DEV):
            bias[b, :, :BLOCK] = jnp.where(offset <= row, 0.0, -jnp.inf)
            for j in range(SLOTS):
                limit = vis_ref[b * SLOTS + j]
                bias[b, :, (1 + j) * BLOCK : (2 + j) * BLOCK] = jnp.where(offset < limit, 0.0, -jnp.inf)
        glat[...] = jnp.zeros_like(glat)
        grope[...] = jnp.zeros_like(grope)

    heads = range(HEADS_STEP)
    nope = [query_ref[:, h * QDIM : h * QDIM + HEAD_DIM] for h in heads]
    rope = [query_ref[:, h * QDIM + HEAD_DIM : (h + 1) * QDIM] for h in heads]
    grad = [grad_ref[:, h * HEAD_DIM : (h + 1) * HEAD_DIM] for h in heads]
    key_up = [key_up_ref[:, h * HEAD_DIM : (h + 1) * HEAD_DIM] for h in heads]
    value_up = [value_up_ref[:, h * HEAD_DIM : (h + 1) * HEAD_DIM] for h in heads]
    absorbed = [dot_nt(nope[h], key_up[h]).astype(bf16) for h in heads]
    mixed_grad = [dot_nt(grad[h], value_up[h]).astype(bf16) for h in heads]

    for b in range(BLOCKS_DEV):
        rows = slice(b * BLOCK, (b + 1) * BLOCK)
        ab = jnp.concatenate([absorbed[h][rows] for h in heads], axis=0)
        rb = jnp.concatenate([rope[h][rows] for h in heads], axis=0)
        mg = jnp.concatenate([mixed_grad[h][rows] for h in heads], axis=0)
        lat = klat[b]
        rop = krope[b]
        mask = jnp.concatenate([bias[b]] * HEADS_STEP, axis=0)
        scores = (dot_nt(ab, lat) + dot_nt(rb, rop)) * scale + mask
        exp_terms = jnp.exp(scores - jnp.max(scores, axis=1, keepdims=True))
        weights = exp_terms * (1.0 / jnp.sum(exp_terms, axis=1, keepdims=True))
        half = weights.astype(bf16)
        weights_ref[b] = half
        weight_grad = dot_nt(mg, lat)
        inner = jnp.sum(weights * weight_grad, axis=1, keepdims=True)
        score_grad = (weights * (weight_grad - inner) * scale).astype(bf16)
        sgrad_ref[b] = score_grad
        both = jnp.concatenate([score_grad, half], axis=0)
        glat[b] += dot_tn(both, jnp.concatenate([ab, mg], axis=0))
        grope[b] += dot_tn(score_grad, rb)

    @pl.when(step == pl.num_programs(0) - 1)
    def _():
        for b in range(BLOCKS_DEV):
            for j in range(1 + SLOTS):
                tile = b if j == 0 else BLOCKS_DEV + b * SLOTS + j - 1
                for y in range(NY):
                    at = j * BLOCK + y * ROWS
                    keep_ref[y, tile, :, :LATENT] = glat[b, at : at + ROWS, :]
                    keep_ref[y, tile, :, LATENT:] = grope[b, at : at + ROWS, :]
                    at = at + HALF
                    send_ref[y, tile, :, :LATENT] = glat[b, at : at + ROWS, :].astype(bf16)
                    send_ref[y, tile, :, LATENT:] = grope[b, at : at + ROWS, :].astype(bf16)


def project_kernel(
    x_ref, query_ref, grad_ref, key_up_ref, value_up_ref, sgrad_ref, weights_ref, klat, krope,
    attn_ref, qgrad_ref, w0_ref, w1_ref, w2_ref, w3_ref,
    wgrad,
):
    heads = range(HEADS_STEP)
    nope = [query_ref[:, h * QDIM : h * QDIM + HEAD_DIM] for h in heads]
    grad = [grad_ref[:, h * HEAD_DIM : (h + 1) * HEAD_DIM] for h in heads]
    key_up = [key_up_ref[:, h * HEAD_DIM : (h + 1) * HEAD_DIM] for h in heads]
    value_up = [value_up_ref[:, h * HEAD_DIM : (h + 1) * HEAD_DIM] for h in heads]
    mixed_parts, full_parts, rope_parts = [], [], []
    for b in range(BLOCKS_DEV):
        score_grad = sgrad_ref[b]
        mixed_parts.append(dot(weights_ref[b], klat[b]).astype(bf16))
        full_parts.append(dot(score_grad, klat[b]).astype(bf16))
        rope_parts.append(dot(score_grad, krope[b]).astype(bf16))

    def head_rows(parts, h):
        return jnp.concatenate([part[h * BLOCK : (h + 1) * BLOCK] for part in parts], axis=0)

    width = HEADS_STEP * HEAD_DIM
    for h in heads:
        mixed = head_rows(mixed_parts, h)
        full = head_rows(full_parts, h)
        attn_ref[:, h * HEAD_DIM : (h + 1) * HEAD_DIM] = dot(mixed, value_up[h]).astype(bf16)
        qgrad_ref[:, h * QDIM : h * QDIM + HEAD_DIM] = dot(full, key_up[h]).astype(bf16)
        qgrad_ref[:, h * QDIM + HEAD_DIM : (h + 1) * QDIM] = head_rows(rope_parts, h)
        at = h * HEAD_DIM
        wgrad[:, at : at + HEAD_DIM] = dot_tn(full, nope[h]).astype(bf16)
        wgrad[:, width + at : width + at + HEAD_DIM] = dot_tn(mixed, grad[h]).astype(bf16)

    for r, out in enumerate((w0_ref, w1_ref, w2_ref, w3_ref)):
        start = pl.multiple_of(((x_ref[0] + r) % NX) * PART, PART)
        out[...] = wgrad[pl.ds(start, PART), :]


def pair_kernel(y_ref, keep_ref, recv_ref, own_ref, s1_ref, s2_ref, s3_ref):
    for r, out in enumerate((own_ref, s1_ref, s2_ref, s3_ref)):
        y = (y_ref[0] + r) % NY
        out[...] = (keep_ref[y] + recv_ref[y].astype(f32)).astype(out.dtype)


def slots_kernel(own_ref, r1_ref, r2_ref, r3_ref, mine_ref, out_ref):
    total = own_ref[...] + r1_ref[...].astype(f32) + r2_ref[...].astype(f32) + r3_ref[...].astype(f32)
    mine_ref[...] = total[:BLOCKS_DEV]
    out_ref[...] = total[BLOCKS_DEV:].astype(bf16)


def column_kernel(x_ref, z_ref, l0, l1, l2, l3, mine_ref, i0, i1, i2, i3, out_ref, acc):
    acc[...] = jnp.zeros_like(acc)
    for b in range(BLOCKS_DEV):
        acc[z_ref[0] * BLOCKS_DEV + b] = mine_ref[b]
    for listed, in_ref in ((l0, i0), (l1, i1), (l2, i2), (l3, i3)):
        for s in range(BLOCKS_DEV * SLOTS):
            block = listed[s]

            @pl.when(block // COLUMN == x_ref[0])
            def _():
                at = block % COLUMN
                acc[at] = acc[at] + in_ref[s].astype(f32)

    for z in range(NZ):
        for b in range(BLOCKS_DEV):
            out_ref[z, b] = acc[z * BLOCKS_DEV + b].astype(bf16)


def line_kernel(in_ref, out_ref):
    total = in_ref[0].astype(f32)
    for z in range(1, NZ):
        total = total + in_ref[z].astype(f32)
    out_ref[...] = total.astype(bf16)


def part_kernel(w0, w1, w2, w3, out_ref):
    for z in range(NZ):
        rows = slice(z * ROWS, (z + 1) * ROWS)
        out_ref[z] = sum(ref[rows].astype(f32) for ref in (w0, w1, w2, w3)).astype(bf16)


def weights_kernel(in_ref, key_ref, value_ref):
    total = sum(in_ref[z].astype(f32) for z in range(NZ))
    for h in range(HEADS_DEV):
        at = (h // HEADS_STEP) * 2 * HEADS_STEP * HEAD_DIM + (h % HEADS_STEP) * HEAD_DIM
        key_ref[:, h, :] = total[:, at : at + HEAD_DIM]
        at = at + HEADS_STEP * HEAD_DIM
        value_ref[:, h, :] = total[:, at : at + HEAD_DIM]


def cores_kernel(core_ref, near_ref, far_ref, out_ref):
    for b in range(BLOCKS_DEV):
        out_ref[b, core_ref[0]] = near_ref[b]
        out_ref[b, 1 - core_ref[0]] = far_ref[b]


def final_kernel(y_ref, i0, i1, i2, i3, latent_ref, gain_ref, out_ref):
    for r, in_ref in enumerate((i0, i1, i2, i3)):
        y = (y_ref[0] - r + NY) % NY
        for b in range(BLOCKS_DEV):
            total = in_ref[b].reshape(NC * ROWS, KV).astype(f32)
            rows = pl.ds(pl.multiple_of(b * BLOCK + y * NC * ROWS, NC * ROWS), NC * ROWS)
            raw = latent_ref[rows, :LATENT].astype(f32)
            inverse = norm_inverse(raw)
            gained = total[:, :LATENT] * gain_ref[...]
            out_ref[rows, :LATENT] = inverse * gained - raw * inverse * inverse * inverse * jnp.mean(
                raw * gained, axis=1, keepdims=True
            )
            out_ref[rows, LATENT:] = total[:, LATENT:]


def call(kernel, out_shape, in_specs, **kw):
    return pl.pallas_call(
        kernel,
        out_shape=out_shape,
        in_specs=in_specs,
        out_specs=kw.pop("out_specs", vmem()),
        compiler_params=pltpu.CompilerParams(vmem_limit_bytes=VMEM_LIMIT),
        **kw,
    )


def shape(*dims, dtype=bf16):
    return jax.ShapeDtypeStruct(dims, dtype)


def exchange(values, axis):
    return lax.all_to_all(values, axis, split_axis=0, concat_axis=0, tiled=True)


def shift(values, axis, count, by):
    return lax.ppermute(values, axis, [(i, (i + by) % count) for i in range(count)])


def swap_cores(values):
    return lax.ppermute(values, "c", [(0, 1), (1, 0)])


def columns(rows, cols):
    return pl.BlockSpec((rows, cols), lambda g: (0, g))


def whole(*dims):
    return pl.BlockSpec(dims, lambda g: (0,) * len(dims))


def cost(flops):
    return pl.CostEstimate(flops=flops, bytes_accessed=8_000_000, transcendentals=0)


def shards(query, latent, norm_gain, key_up, value_up, out_grad, ancestors, visible):
    def index(axis):
        return lax.axis_index(axis).astype(jnp.int32).reshape(1)

    core, x, y, z = index("c"), index("x"), index("y"), index("z")
    share = y * NC + core
    gain = norm_gain.reshape(1, LATENT)
    listed = ancestors.reshape(BLOCKS_DEV * SLOTS)
    limits = visible.reshape(BLOCKS_DEV * SLOTS)
    slots = BLOCKS_DEV * SLOTS
    lists = [listed] + [shift(listed, "x", NX, -r) for r in range(1, NX)]

    mine = call(share_kernel, shape(NZ, BLOCKS_DEV, ROWS, KV), [smem(), vmem(), vmem()])(share, latent, gain)
    key_up_flat = key_up.reshape(LATENT, HEADS_DEV * HEAD_DIM)
    value_up_flat = value_up.reshape(LATENT, HEADS_DEV * HEAD_DIM)
    column = exchange(mine, "z").reshape(COLUMN, ROWS, KV)
    column = call(spread_kernel, shape(NX, slots, ROWS, KV), [smem()] * 5 + [vmem()])(x, *lists, column)
    column, key_up_flat, value_up_flat = lax.optimization_barrier((column, key_up_flat, value_up_flat))
    column = exchange(column, "x")
    picked = call(select_kernel, shape(NY, slots, ROWS, KV), [smem(), vmem()])(listed, column)
    near = exchange(picked, "y")
    far = swap_cores(near)

    tokens = query.shape[0]
    steps = HEADS_DEV // HEADS_STEP
    width = HEADS_STEP * HEAD_DIM
    wcols = 2 * HEADS_DEV * HEAD_DIM
    rows = HEADS_DEV * BLOCK
    lat_keys, rope_keys = (BLOCKS_DEV, KEYS, LATENT), (BLOCKS_DEV, KEYS, ROPE)
    tiles = (NY, TILES, ROWS, KV)
    operands = (query, out_grad, key_up_flat, value_up_flat)
    operand_specs = [columns(tokens, HEADS_STEP * QDIM), columns(tokens, width), columns(LATENT, width), columns(LATENT, width)]
    by_rows = pl.BlockSpec((BLOCKS_DEV, HEADS_STEP * BLOCK, KEYS), lambda g: (0, g, 0))
    score_grad, weights, klat, krope, keep, send = call(
        attend_kernel,
        (shape(BLOCKS_DEV, rows, KEYS),) * 2 + (shape(*lat_keys), shape(*rope_keys), shape(*tiles, dtype=f32), shape(*tiles)),
        [smem()] * 2 + operand_specs + [whole(tokens, KV), whole(1, LATENT)] + [whole(NY, slots, ROWS, KV)] * 2,
        out_specs=(by_rows, by_rows, whole(*lat_keys), whole(*rope_keys), whole(*tiles), whole(*tiles)),
        grid=(steps,),
        scratch_shapes=[
            pltpu.VMEM((BLOCKS_DEV, BLOCK, KEYS), f32),
            pltpu.VMEM(lat_keys, f32),
            pltpu.VMEM(rope_keys, f32),
        ],
        cost_estimate=cost(6_200_000_000),
    )(core, limits, *operands, latent, gain, near, far)

    own, s1, s2, s3 = call(
        pair_kernel,
        (shape(TILES, ROWS, KV, dtype=f32),) + (shape(TILES, ROWS, KV),) * 3,
        [smem(), vmem(), vmem()],
        out_specs=(vmem(),) * 4,
    )(y, keep, swap_cores(send))
    others = [shift(s, "y", NY, r) for r, s in ((1, s1), (2, s2), (3, s3))]
    own, score_grad = lax.optimization_barrier((own, score_grad))
    attn_out, query_grad, *wgrads = call(
        project_kernel,
        (shape(tokens, HEADS_DEV * HEAD_DIM), shape(tokens, HEADS_DEV * QDIM)) + (shape(PART, wcols),) * NX,
        [smem()] + operand_specs + [by_rows, by_rows, whole(*lat_keys), whole(*rope_keys)],
        out_specs=(columns(tokens, width), columns(tokens, HEADS_STEP * QDIM)) + (columns(PART, 2 * width),) * NX,
        grid=(steps,),
        scratch_shapes=[pltpu.VMEM((LATENT, 2 * width), bf16)],
        cost_estimate=cost(4_000_000_000),
    )(x, *operands, score_grad, weights, klat, krope)
    parts = [shift(w, "x", NX, r) for r, w in enumerate(wgrads) if r > 0]
    *others, wgrads[0] = lax.optimization_barrier((*others, wgrads[0]))
    own, spread = call(
        slots_kernel,
        (shape(BLOCKS_DEV, ROWS, KV, dtype=f32), shape(slots, ROWS, KV)),
        [vmem()] * 4,
        out_specs=(vmem(), vmem()),
    )(own, *others)
    others = [shift(spread, "x", NX, -r) for r in range(1, NX)]
    line = call(
        column_kernel,
        shape(NZ, BLOCKS_DEV, ROWS, KV),
        [smem()] * 6 + [vmem()] * 5,
        scratch_shapes=[pltpu.VMEM((COLUMN, ROWS, KV), f32)],
    )(x, z, *lists, own, spread, *others)
    line = exchange(line, "z")
    line, *parts = lax.optimization_barrier((line, *parts))
    part = call(part_kernel, shape(NZ, ROWS, wcols), [vmem()] * NX)(wgrads[0], *parts)
    part = exchange(part, "z")
    total = call(line_kernel, shape(BLOCKS_DEV, ROWS, KV), [vmem()])(line)
    total = call(cores_kernel, shape(BLOCKS_DEV, NC, ROWS, KV), [smem(), vmem(), vmem()])(
        core, total, swap_cores(total)
    )
    others = [shift(total, "y", NY, r) for r in range(1, NY)]
    latent_grad = call(final_kernel, shape(tokens, KV, dtype=f32), [smem()] + [vmem()] * 6)(
        y, total, *others, latent, gain
    )
    grad_shape = shape(PART // NZ, HEADS_DEV, HEAD_DIM, dtype=f32)
    key_up_grad, value_up_grad = call(
        weights_kernel, (grad_shape, grad_shape), [vmem()], out_specs=(vmem(), vmem())
    )(part)
    return attn_out, query_grad, latent_grad, key_up_grad, value_up_grad


def solution(mesh):
    grid = Mesh(mesh.devices.reshape(NX, NZ, NY, NC), ("x", "z", "y", "c"))
    pos, head = ("x", "z"), ("y", "c")
    return jax.shard_map(
        shards,
        mesh=grid,
        in_specs=(
            P(pos, head),
            P(pos, None),
            P(),
            P(None, head, None),
            P(None, head, None),
            P(pos, head),
            P(pos, None),
            P(pos, None),
        ),
        out_specs=(
            P(pos, head),
            P(pos, head),
            P(pos, None),
            P(pos, head, None),
            P(pos, head, None),
        ),
        check_vma=False,
    )
```

```python
import functools
import math

import jax
import jax.numpy as jnp
from jax import lax
from jax.experimental import pallas as pl
from jax.experimental.pallas import tpu as pltpu
from jax.sharding import Mesh
from jax.sharding import PartitionSpec as P

LATENT = 512
ROPE = 64
KV = LATENT + ROPE
HEAD_DIM = 128
QDIM = HEAD_DIM + ROPE
BLOCK = 128
SLOTS = 4
BLOCKS_DEV = 2
NX, NZ, NY, NC = 4, 8, 4, 2
SHARES = NY * NC
ROWS = BLOCK // SHARES
HALF = NY * ROWS
HEADS_DEV = 8
TILES = BLOCKS_DEV * (1 + SLOTS)
KEYS = (1 + SLOTS) * BLOCK
COLUMN = NZ * BLOCKS_DEV
PART = LATENT // NX
HEADS_STEP = 4
norm_epsilon = 1e-06

bf16 = jnp.bfloat16
f32 = jnp.float32
VMEM_LIMIT = 48 * 1024 * 1024


def dot(a, b):
    return lax.dot_general(a, b, (((1,), (0,)), ((), ())), preferred_element_type=f32)


def dot_nt(a, b):
    return lax.dot_general(a, b, (((1,), (1,)), ((), ())), preferred_element_type=f32)


def dot_tn(a, b):
    return lax.dot_general(a, b, (((0,), (0,)), ((), ())), preferred_element_type=f32)


def smem():
    return pl.BlockSpec(memory_space=pltpu.SMEM)


def vmem():
    return pl.BlockSpec(memory_space=pltpu.VMEM)


def norm_inverse(raw):
    return lax.rsqrt(jnp.mean(raw * raw, axis=1, keepdims=True) + norm_epsilon)


def share_kernel(share_ref, latent_ref, gain_ref, out_ref):
    for b in range(BLOCKS_DEV):
        start = pl.multiple_of(b * BLOCK + share_ref[0] * ROWS, ROWS)
        raw = latent_ref[pl.ds(start, ROWS), :LATENT].astype(f32)
        keys = (raw * norm_inverse(raw) * gain_ref[...]).astype(bf16)
        rope = latent_ref[pl.ds(start, ROWS), LATENT:]
        for z in range(NZ):
            out_ref[z, b, :, :LATENT] = keys
            out_ref[z, b, :, LATENT:] = rope


def spread_kernel(l0, l1, l2, l3, column_ref, o0, o1, o2, o3):
    for listed, out in ((l0, o0), (l1, o1), (l2, o2), (l3, o3)):
        for s in range(BLOCKS_DEV * SLOTS):
            out[s] = column_ref[listed[s] % COLUMN]


def select_kernel(x_ref, listed_ref, i0, i1, i2, i3, out_ref):
    for s in range(BLOCKS_DEV * SLOTS):
        back = (x_ref[0] - listed_ref[s] // COLUMN + NX) % NX
        for r, in_ref in enumerate((i0, i1, i2, i3)):

            @pl.when(back == r)
            def _():
                out_ref[s] = in_ref[s]


def attend_kernel(
    core_ref, y_ref, vis_ref, query_ref, grad_ref, key_up_ref, value_up_ref, latent_ref, gain_ref,
    n0, n1, n2, n3, f0, f1, f2, f3,
    sgrad_ref, weights_ref, klat, krope, keep_ref, send_ref,
    bias, glat, grope, own,
):
    step = pl.program_id(0)
    core = core_ref[0]
    scale = 1.0 / math.sqrt(QDIM)

    @pl.when(step == 0)
    def _():
        raw = latent_ref[:, :LATENT].astype(f32)
        own[...] = (raw * norm_inverse(raw) * gain_ref[...]).astype(bf16)
        for side, pieces in enumerate(((n0, n1, n2, n3), (f0, f1, f2, f3))):
            for r, piece in enumerate(pieces):
                at = side * HALF + r * ROWS
                owner = (y_ref[0] - r + NY) % NY * NC + (core + side) % NC
                for b in range(BLOCKS_DEV):
                    rows = pl.ds(pl.multiple_of(b * BLOCK + owner * ROWS, ROWS), ROWS)
                    klat[b, at : at + ROWS, :] = own[rows, :]
                    krope[b, at : at + ROWS, :] = latent_ref[rows, LATENT:]
                    for j in range(SLOTS):
                        to = (1 + j) * BLOCK + at
                        klat[b, to : to + ROWS, :] = piece[b * SLOTS + j, :, :LATENT]
                        krope[b, to : to + ROWS, :] = piece[b * SLOTS + j, :, LATENT:]
        col = lax.broadcasted_iota(jnp.int32, (BLOCK, BLOCK), 1)
        row = lax.broadcasted_iota(jnp.int32, (BLOCK, BLOCK), 0)
        side = jnp.where(col >= HALF, 1, 0)
        rest = col - side * HALF
        piece = (y_ref[0] - rest // ROWS + NY) % NY
        owner = jnp.where(core == 0, side, 1 - side)
        offset = (piece * NC + owner) * ROWS + rest % ROWS
        for b in range(BLOCKS_DEV):
            bias[b, :, :BLOCK] = jnp.where(offset <= row, 0.0, -jnp.inf)
            for j in range(SLOTS):
                limit = vis_ref[b * SLOTS + j]
                bias[b, :, (1 + j) * BLOCK : (2 + j) * BLOCK] = jnp.where(offset < limit, 0.0, -jnp.inf)
        glat[...] = jnp.zeros_like(glat)
        grope[...] = jnp.zeros_like(grope)

    heads = range(HEADS_STEP)
    nope = [query_ref[:, h * QDIM : h * QDIM + HEAD_DIM] for h in heads]
    rope = [query_ref[:, h * QDIM + HEAD_DIM : (h + 1) * QDIM] for h in heads]
    grad = [grad_ref[:, h * HEAD_DIM : (h + 1) * HEAD_DIM] for h in heads]
    key_up = [key_up_ref[:, h * HEAD_DIM : (h + 1) * HEAD_DIM] for h in heads]
    value_up = [value_up_ref[:, h * HEAD_DIM : (h + 1) * HEAD_DIM] for h in heads]
    absorbed = [dot_nt(nope[h], key_up[h]).astype(bf16) for h in heads]
    mixed_grad = [dot_nt(grad[h], value_up[h]).astype(bf16) for h in heads]

    for b in range(BLOCKS_DEV):
        rows = slice(b * BLOCK, (b + 1) * BLOCK)
        ab = jnp.concatenate([absorbed[h][rows] for h in heads], axis=0)
        rb = jnp.concatenate([rope[h][rows] for h in heads], axis=0)
        mg = jnp.concatenate([mixed_grad[h][rows] for h in heads], axis=0)
        lat = klat[b]
        rop = krope[b]
        mask = jnp.concatenate([bias[b]] * HEADS_STEP, axis=0)
        scores = (dot_nt(ab, lat) + dot_nt(rb, rop)) * scale + mask
        exp_terms = jnp.exp(scores - jnp.max(scores, axis=1, keepdims=True))
        weights = exp_terms * (1.0 / jnp.sum(exp_terms, axis=1, keepdims=True))
        half = weights.astype(bf16)
        weights_ref[b] = half
        weight_grad = dot_nt(mg, lat)
        inner = jnp.sum(weights * weight_grad, axis=1, keepdims=True)
        score_grad = (weights * (weight_grad - inner) * scale).astype(bf16)
        sgrad_ref[b] = score_grad
        both = jnp.concatenate([score_grad, half], axis=0)
        glat[b] += dot_tn(both, jnp.concatenate([ab, mg], axis=0))
        grope[b] += dot_tn(score_grad, rb)

    @pl.when(step == pl.num_programs(0) - 1)
    def _():
        for b in range(BLOCKS_DEV):
            for j in range(1 + SLOTS):
                tile = b if j == 0 else BLOCKS_DEV + b * SLOTS + j - 1
                for y in range(NY):
                    at = j * BLOCK + y * ROWS
                    keep_ref[y, tile, :, :LATENT] = glat[b, at : at + ROWS, :]
                    keep_ref[y, tile, :, LATENT:] = grope[b, at : at + ROWS, :]
                    at = at + HALF
                    send_ref[y, tile, :, :LATENT] = glat[b, at : at + ROWS, :].astype(bf16)
                    send_ref[y, tile, :, LATENT:] = grope[b, at : at + ROWS, :].astype(bf16)


def project_kernel(
    x_ref, query_ref, grad_ref, key_up_ref, value_up_ref, sgrad_ref, weights_ref, klat, krope,
    attn_ref, qgrad_ref, w0_ref, w1_ref, w2_ref, w3_ref,
    wgrad,
):
    heads = range(HEADS_STEP)
    nope = [query_ref[:, h * QDIM : h * QDIM + HEAD_DIM] for h in heads]
    grad = [grad_ref[:, h * HEAD_DIM : (h + 1) * HEAD_DIM] for h in heads]
    key_up = [key_up_ref[:, h * HEAD_DIM : (h + 1) * HEAD_DIM] for h in heads]
    value_up = [value_up_ref[:, h * HEAD_DIM : (h + 1) * HEAD_DIM] for h in heads]
    mixed_parts, full_parts, rope_parts = [], [], []
    for b in range(BLOCKS_DEV):
        score_grad = sgrad_ref[b]
        mixed_parts.append(dot(weights_ref[b], klat[b]).astype(bf16))
        full_parts.append(dot(score_grad, klat[b]).astype(bf16))
        rope_parts.append(dot(score_grad, krope[b]).astype(bf16))

    def head_rows(parts, h):
        return jnp.concatenate([part[h * BLOCK : (h + 1) * BLOCK] for part in parts], axis=0)

    width = HEADS_STEP * HEAD_DIM
    for h in heads:
        mixed = head_rows(mixed_parts, h)
        full = head_rows(full_parts, h)
        attn_ref[:, h * HEAD_DIM : (h + 1) * HEAD_DIM] = dot(mixed, value_up[h]).astype(bf16)
        qgrad_ref[:, h * QDIM : h * QDIM + HEAD_DIM] = dot(full, key_up[h]).astype(bf16)
        qgrad_ref[:, h * QDIM + HEAD_DIM : (h + 1) * QDIM] = head_rows(rope_parts, h)
        at = h * HEAD_DIM
        wgrad[:, at : at + HEAD_DIM] = dot_tn(full, nope[h]).astype(bf16)
        wgrad[:, width + at : width + at + HEAD_DIM] = dot_tn(mixed, grad[h]).astype(bf16)

    for r, out in enumerate((w0_ref, w1_ref, w2_ref, w3_ref)):
        start = pl.multiple_of(((x_ref[0] + r) % NX) * PART, PART)
        out[...] = wgrad[pl.ds(start, PART), :]


def pair_kernel(keep_ref, recv_ref, own_ref, s1_ref, s2_ref, s3_ref):
    for r, out in enumerate((own_ref, s1_ref, s2_ref, s3_ref)):
        y = (NY - r) % NY
        out[...] = (keep_ref[y] + recv_ref[y].astype(f32)).astype(out.dtype)


def slots_kernel(own_ref, r1_ref, r2_ref, r3_ref, mine_ref, out_ref):
    total = own_ref[...] + r1_ref[...].astype(f32) + r2_ref[...].astype(f32) + r3_ref[...].astype(f32)
    mine_ref[...] = total[:BLOCKS_DEV]
    out_ref[...] = total[BLOCKS_DEV:].astype(bf16)


def column_kernel(x_ref, z_ref, l0, l1, l2, l3, mine_ref, i0, i1, i2, i3, out_ref, acc):
    acc[...] = jnp.zeros_like(acc)
    for b in range(BLOCKS_DEV):
        acc[z_ref[0] * BLOCKS_DEV + b] = mine_ref[b]
    for listed, in_ref in ((l0, i0), (l1, i1), (l2, i2), (l3, i3)):
        for s in range(BLOCKS_DEV * SLOTS):
            block = listed[s]

            @pl.when(block // COLUMN == x_ref[0])
            def _():
                at = block % COLUMN
                acc[at] = acc[at] + in_ref[s].astype(f32)

    for z in range(NZ):
        for b in range(BLOCKS_DEV):
            out_ref[z, b] = acc[z * BLOCKS_DEV + b].astype(bf16)


def line_kernel(in_ref, out_ref):
    total = in_ref[0].astype(f32)
    for z in range(1, NZ):
        total = total + in_ref[z].astype(f32)
    out_ref[...] = total.astype(bf16)


def part_kernel(w0, w1, w2, w3, out_ref):
    for z in range(NZ):
        rows = slice(z * ROWS, (z + 1) * ROWS)
        out_ref[z] = sum(ref[rows].astype(f32) for ref in (w0, w1, w2, w3)).astype(bf16)


def weights_kernel(in_ref, key_ref, value_ref):
    total = sum(in_ref[z].astype(f32) for z in range(NZ))
    for h in range(HEADS_DEV):
        at = (h // HEADS_STEP) * 2 * HEADS_STEP * HEAD_DIM + (h % HEADS_STEP) * HEAD_DIM
        key_ref[:, h, :] = total[:, at : at + HEAD_DIM]
        at = at + HEADS_STEP * HEAD_DIM
        value_ref[:, h, :] = total[:, at : at + HEAD_DIM]


def cores_kernel(core_ref, near_ref, far_ref, out_ref):
    for b in range(BLOCKS_DEV):
        out_ref[b, core_ref[0]] = near_ref[b]
        out_ref[b, 1 - core_ref[0]] = far_ref[b]


def final_kernel(y_ref, i0, i1, i2, i3, latent_ref, gain_ref, out_ref):
    for r, in_ref in enumerate((i0, i1, i2, i3)):
        y = (y_ref[0] - r + NY) % NY
        for b in range(BLOCKS_DEV):
            total = in_ref[b].reshape(NC * ROWS, KV).astype(f32)
            rows = pl.ds(pl.multiple_of(b * BLOCK + y * NC * ROWS, NC * ROWS), NC * ROWS)
            raw = latent_ref[rows, :LATENT].astype(f32)
            inverse = norm_inverse(raw)
            gained = total[:, :LATENT] * gain_ref[...]
            out_ref[rows, :LATENT] = inverse * gained - raw * inverse * inverse * inverse * jnp.mean(
                raw * gained, axis=1, keepdims=True
            )
            out_ref[rows, LATENT:] = total[:, LATENT:]


def call(kernel, out_shape, in_specs, limit=VMEM_LIMIT, **kw):
    return pl.pallas_call(
        kernel,
        out_shape=out_shape,
        in_specs=in_specs,
        out_specs=kw.pop("out_specs", vmem()),
        compiler_params=pltpu.CompilerParams(vmem_limit_bytes=limit),
        **kw,
    )


def shape(*dims, dtype=bf16):
    return jax.ShapeDtypeStruct(dims, dtype)


def exchange(values, axis):
    return lax.all_to_all(values, axis, split_axis=0, concat_axis=0, tiled=True)


def shift(values, axis, count, by):
    return lax.ppermute(values, axis, [(i, (i + by) % count) for i in range(count)])


def in_hbm(values):
    return pltpu.with_memory_space_constraint(values, pltpu.HBM)


def swap_cores(values):
    return lax.ppermute(values, "c", [(0, 1), (1, 0)])


def columns(rows, cols):
    return pl.BlockSpec((rows, cols), lambda g: (0, g))


def whole(*dims):
    return pl.BlockSpec(dims, lambda g: (0,) * len(dims))


def cost(flops):
    return pl.CostEstimate(flops=flops, bytes_accessed=8_000_000, transcendentals=0)


def shards(query, latent, norm_gain, key_up, value_up, out_grad, ancestors, visible):
    def index(axis):
        return lax.axis_index(axis).astype(jnp.int32).reshape(1)

    core, x, y, z = index("c"), index("x"), index("y"), index("z")
    share = y * NC + core
    gain = norm_gain.reshape(1, LATENT)
    listed = ancestors.reshape(BLOCKS_DEV * SLOTS)
    limits = visible.reshape(BLOCKS_DEV * SLOTS)
    slots = BLOCKS_DEV * SLOTS
    lists = [listed] + [shift(listed, "x", NX, -r) for r in range(1, NX)]

    mine = call(share_kernel, shape(NZ, BLOCKS_DEV, ROWS, KV), [smem(), vmem(), vmem()])(share, latent, gain)
    key_up_flat = key_up.reshape(LATENT, HEADS_DEV * HEAD_DIM)
    value_up_flat = value_up.reshape(LATENT, HEADS_DEV * HEAD_DIM)
    column = exchange(mine, "z").reshape(COLUMN, ROWS, KV)
    column, key_up_flat, value_up_flat = lax.optimization_barrier((column, key_up_flat, value_up_flat))
    tile_list = shape(slots, ROWS, KV)
    sent = call(spread_kernel, (tile_list,) * NX, [smem()] * NX + [vmem()], out_specs=(vmem(),) * NX)(*lists, column)
    got = [sent[0]] + [shift(sent[r], "x", NX, r) for r in range(1, NX)]
    picked = call(select_kernel, tile_list, [smem()] * 2 + [vmem()] * NX)(x, listed, *got)
    near = [picked] + [shift(picked, "y", NY, r) for r in range(1, NY)]
    far = [swap_cores(piece) for piece in near]

    tokens = query.shape[0]
    steps = HEADS_DEV // HEADS_STEP
    width = HEADS_STEP * HEAD_DIM
    wcols = 2 * HEADS_DEV * HEAD_DIM
    rows = HEADS_DEV * BLOCK
    lat_keys, rope_keys = (BLOCKS_DEV, KEYS, LATENT), (BLOCKS_DEV, KEYS, ROPE)
    tiles = (NY, TILES, ROWS, KV)
    query, out_grad = in_hbm(query), in_hbm(out_grad)
    operands = (query, out_grad, key_up_flat, value_up_flat)
    operand_specs = [columns(tokens, HEADS_STEP * QDIM), columns(tokens, width), columns(LATENT, width), columns(LATENT, width)]
    by_rows = pl.BlockSpec((BLOCKS_DEV, HEADS_STEP * BLOCK, KEYS), lambda g: (0, g, 0))
    score_grad, weights, klat, krope, keep, send = call(
        attend_kernel,
        (pltpu.HBM((BLOCKS_DEV, rows, KEYS), bf16),) * 2
        + (pltpu.HBM(lat_keys, bf16), pltpu.HBM(rope_keys, bf16), pltpu.VMEM(tiles, f32), pltpu.HBM(tiles, bf16)),
        [smem()] * 3 + operand_specs + [whole(tokens, KV), whole(1, LATENT)] + [whole(slots, ROWS, KV)] * (2 * NY),
        out_specs=(by_rows, by_rows, whole(*lat_keys), whole(*rope_keys), whole(*tiles), whole(*tiles)),
        grid=(steps,),
        scratch_shapes=[
            pltpu.VMEM((BLOCKS_DEV, BLOCK, KEYS), f32),
            pltpu.VMEM(lat_keys, f32),
            pltpu.VMEM(rope_keys, f32),
            pltpu.VMEM((tokens, LATENT), bf16),
        ],
        cost_estimate=cost(6_200_000_000),
        limit=44 * 1024 * 1024,
    )(core, y, limits, *operands, latent, gain, *near, *far)

    own, s1, s2, s3 = call(
        pair_kernel,
        (shape(TILES, ROWS, KV, dtype=f32),) + (shape(TILES, ROWS, KV),) * 3,
        [vmem(), vmem()],
        out_specs=(vmem(),) * 4,
    )(keep, swap_cores(send))
    others = [shift(s, "y", NY, r) for r, s in ((1, s1), (2, s2), (3, s3))]
    own, score_grad = lax.optimization_barrier((own, score_grad))
    attn_out, query_grad, *wgrads = call(
        project_kernel,
        (shape(tokens, HEADS_DEV * HEAD_DIM), shape(tokens, HEADS_DEV * QDIM)) + (shape(PART, wcols),) * NX,
        [smem()] + operand_specs + [by_rows, by_rows, whole(*lat_keys), whole(*rope_keys)],
        out_specs=(columns(tokens, width), columns(tokens, HEADS_STEP * QDIM)) + (columns(PART, 2 * width),) * NX,
        grid=(steps,),
        scratch_shapes=[pltpu.VMEM((LATENT, 2 * width), bf16)],
        cost_estimate=cost(4_000_000_000),
    )(x, *operands, in_hbm(score_grad), in_hbm(weights), in_hbm(klat), in_hbm(krope))
    parts = [shift(w, "x", NX, r) for r, w in enumerate(wgrads) if r > 0]
    *others, wgrads[0] = lax.optimization_barrier((*others, wgrads[0]))
    own, spread = call(
        slots_kernel,
        (shape(BLOCKS_DEV, ROWS, KV, dtype=f32), shape(slots, ROWS, KV)),
        [vmem()] * 4,
        out_specs=(vmem(), vmem()),
    )(own, *others)
    others = [shift(spread, "x", NX, -r) for r in range(1, NX)]
    line = call(
        column_kernel,
        shape(NZ, BLOCKS_DEV, ROWS, KV),
        [smem()] * 6 + [vmem()] * 5,
        scratch_shapes=[pltpu.VMEM((COLUMN, ROWS, KV), f32)],
    )(x, z, *lists, own, spread, *others)
    line = exchange(line, "z")
    part = call(part_kernel, shape(NZ, ROWS, wcols), [vmem()] * NX)(wgrads[0], *parts)
    part = exchange(part, "z")
    total = call(line_kernel, shape(BLOCKS_DEV, ROWS, KV), [vmem()])(line)
    total = call(cores_kernel, shape(BLOCKS_DEV, NC, ROWS, KV), [smem(), vmem(), vmem()])(
        core, total, swap_cores(total)
    )
    others = [shift(total, "y", NY, r) for r in range(1, NY)]
    latent_grad = call(final_kernel, shape(tokens, KV, dtype=f32), [smem()] + [vmem()] * 6)(
        y, total, *others, latent, gain
    )
    grad_shape = shape(PART // NZ, HEADS_DEV, HEAD_DIM, dtype=f32)
    key_up_grad, value_up_grad = call(
        weights_kernel, (grad_shape, grad_shape), [vmem()], out_specs=(vmem(), vmem())
    )(part)
    return attn_out, query_grad, latent_grad, key_up_grad, value_up_grad


def solution(mesh):
    grid = Mesh(mesh.devices.reshape(NX, NZ, NY, NC), ("x", "z", "y", "c"))
    pos, head = ("x", "z"), ("y", "c")
    return jax.shard_map(
        shards,
        mesh=grid,
        in_specs=(
            P(pos, head),
            P(pos, None),
            P(),
            P(None, head, None),
            P(None, head, None),
            P(pos, head),
            P(pos, None),
            P(pos, None),
        ),
        out_specs=(
            P(pos, head),
            P(pos, head),
            P(pos, None),
            P(pos, head, None),
            P(pos, head, None),
        ),
        check_vma=False,
    )
```

```python
import functools
import math

import jax
import jax.numpy as jnp
from jax import lax
from jax.experimental import pallas as pl
from jax.experimental.pallas import tpu as pltpu
from jax.sharding import Mesh
from jax.sharding import PartitionSpec as P

LATENT = 512
ROPE = 64
KV = LATENT + ROPE
HEAD_DIM = 128
QDIM = HEAD_DIM + ROPE
BLOCK = 128
SLOTS = 4
BLOCKS_DEV = 2
NX, NZ, NY, NC = 4, 8, 4, 2
SHARES = NY * NC
ROWS = BLOCK // SHARES
HALF = NY * ROWS
HEADS_DEV = 8
TILES = BLOCKS_DEV * (1 + SLOTS)
KEYS = (1 + SLOTS) * BLOCK
COLUMN = NZ * BLOCKS_DEV
PART = LATENT // NX
HEADS_STEP = 4
norm_epsilon = 1e-06

bf16 = jnp.bfloat16
f32 = jnp.float32
VMEM_LIMIT = 48 * 1024 * 1024


def dot(a, b):
    return lax.dot_general(a, b, (((1,), (0,)), ((), ())), preferred_element_type=f32)


def dot_nt(a, b):
    return lax.dot_general(a, b, (((1,), (1,)), ((), ())), preferred_element_type=f32)


def dot_tn(a, b):
    return lax.dot_general(a, b, (((0,), (0,)), ((), ())), preferred_element_type=f32)


def smem():
    return pl.BlockSpec(memory_space=pltpu.SMEM)


def vmem():
    return pl.BlockSpec(memory_space=pltpu.VMEM)


def norm_inverse(raw):
    return lax.rsqrt(jnp.mean(raw * raw, axis=1, keepdims=True) + norm_epsilon)


def share_kernel(share_ref, latent_ref, gain_ref, out_ref):
    for b in range(BLOCKS_DEV):
        start = pl.multiple_of(b * BLOCK + share_ref[0] * ROWS, ROWS)
        raw = latent_ref[pl.ds(start, ROWS), :LATENT].astype(f32)
        keys = (raw * norm_inverse(raw) * gain_ref[...]).astype(bf16)
        rope = latent_ref[pl.ds(start, ROWS), LATENT:]
        for z in range(NZ):
            out_ref[z, b, :, :LATENT] = keys
            out_ref[z, b, :, LATENT:] = rope


def spread_kernel(l0, l1, l2, l3, column_ref, o0, o1, o2, o3):
    for listed, out in ((l0, o0), (l1, o1), (l2, o2), (l3, o3)):
        for s in range(BLOCKS_DEV * SLOTS):
            out[s] = column_ref[listed[s] % COLUMN]


def select_kernel(x_ref, listed_ref, i0, i1, i2, i3, out_ref):
    for s in range(BLOCKS_DEV * SLOTS):
        back = (x_ref[0] - listed_ref[s] // COLUMN + NX) % NX
        for r, in_ref in enumerate((i0, i1, i2, i3)):

            @pl.when(back == r)
            def _():
                out_ref[s] = in_ref[s]


def attend_kernel(
    core_ref, y_ref, vis_ref, query_ref, grad_ref, key_up_ref, value_up_ref, latent_ref, gain_ref,
    n0, n1, n2, n3, f0, f1, f2, f3,
    sgrad_ref, weights_ref, klat, krope, keep_ref, send_ref,
    bias, glat, grope, own,
):
    step = pl.program_id(0)
    core = core_ref[0]
    scale = 1.0 / math.sqrt(QDIM)

    @pl.when(step == 0)
    def _():
        raw = latent_ref[:, :LATENT].astype(f32)
        own[...] = (raw * norm_inverse(raw) * gain_ref[...]).astype(bf16)
        for side, pieces in enumerate(((n0, n1, n2, n3), (f0, f1, f2, f3))):
            for r, piece in enumerate(pieces):
                at = side * HALF + r * ROWS
                owner = (y_ref[0] - r + NY) % NY * NC + (core + side) % NC
                for b in range(BLOCKS_DEV):
                    rows = pl.ds(pl.multiple_of(b * BLOCK + owner * ROWS, ROWS), ROWS)
                    klat[b, at : at + ROWS, :] = own[rows, :]
                    krope[b, at : at + ROWS, :] = latent_ref[rows, LATENT:]
                    for j in range(SLOTS):
                        to = (1 + j) * BLOCK + at
                        klat[b, to : to + ROWS, :] = piece[b * SLOTS + j, :, :LATENT]
                        krope[b, to : to + ROWS, :] = piece[b * SLOTS + j, :, LATENT:]
        col = lax.broadcasted_iota(jnp.int32, (BLOCK, BLOCK), 1)
        row = lax.broadcasted_iota(jnp.int32, (BLOCK, BLOCK), 0)
        side = jnp.where(col >= HALF, 1, 0)
        rest = col - side * HALF
        piece = (y_ref[0] - rest // ROWS + NY) % NY
        owner = jnp.where(core == 0, side, 1 - side)
        offset = (piece * NC + owner) * ROWS + rest % ROWS
        for b in range(BLOCKS_DEV):
            bias[b, :, :BLOCK] = jnp.where(offset <= row, 0.0, -jnp.inf)
            for j in range(SLOTS):
                limit = vis_ref[b * SLOTS + j]
                bias[b, :, (1 + j) * BLOCK : (2 + j) * BLOCK] = jnp.where(offset < limit, 0.0, -jnp.inf)
        glat[...] = jnp.zeros_like(glat)
        grope[...] = jnp.zeros_like(grope)

    heads = range(HEADS_STEP)
    nope = [query_ref[:, h * QDIM : h * QDIM + HEAD_DIM] for h in heads]
    rope = [query_ref[:, h * QDIM + HEAD_DIM : (h + 1) * QDIM] for h in heads]
    grad = [grad_ref[:, h * HEAD_DIM : (h + 1) * HEAD_DIM] for h in heads]
    key_up = [key_up_ref[:, h * HEAD_DIM : (h + 1) * HEAD_DIM] for h in heads]
    value_up = [value_up_ref[:, h * HEAD_DIM : (h + 1) * HEAD_DIM] for h in heads]
    absorbed = [dot_nt(nope[h], key_up[h]).astype(bf16) for h in heads]
    mixed_grad = [dot_nt(grad[h], value_up[h]).astype(bf16) for h in heads]

    staged = []
    for b in range(BLOCKS_DEV):
        rows = slice(b * BLOCK, (b + 1) * BLOCK)
        ab = jnp.concatenate([absorbed[h][rows] for h in heads], axis=0)
        rb = jnp.concatenate([rope[h][rows] for h in heads], axis=0)
        mg = jnp.concatenate([mixed_grad[h][rows] for h in heads], axis=0)
        scores = dot_nt(ab, klat[b]) + dot_nt(rb, krope[b])
        staged.append((ab, rb, mg, scores, dot_nt(mg, klat[b])))
    for b, (ab, rb, mg, scores, weight_grad) in enumerate(staged):
        mask = jnp.concatenate([bias[b]] * HEADS_STEP, axis=0)
        scores = scores * (scale * math.log2(math.e)) + mask
        exp_terms = jnp.exp2(scores - jnp.max(scores, axis=1, keepdims=True))
        weights = exp_terms * (1.0 / jnp.sum(exp_terms, axis=1, keepdims=True))
        half = weights.astype(bf16)
        weights_ref[b] = half
        inner = jnp.sum(weights * weight_grad, axis=1, keepdims=True)
        score_grad = (weights * (weight_grad - inner) * scale).astype(bf16)
        sgrad_ref[b] = score_grad
        both = jnp.concatenate([score_grad, half], axis=0)
        glat[b] += dot_tn(both, jnp.concatenate([ab, mg], axis=0))
        grope[b] += dot_tn(score_grad, rb)

    @pl.when(step == pl.num_programs(0) - 1)
    def _():
        for b in range(BLOCKS_DEV):
            for j in range(1 + SLOTS):
                tile = b if j == 0 else BLOCKS_DEV + b * SLOTS + j - 1
                for y in range(NY):
                    at = j * BLOCK + y * ROWS
                    keep_ref[y, tile, :, :LATENT] = glat[b, at : at + ROWS, :]
                    keep_ref[y, tile, :, LATENT:] = grope[b, at : at + ROWS, :]
                    at = at + HALF
                    send_ref[y, tile, :, :LATENT] = glat[b, at : at + ROWS, :].astype(bf16)
                    send_ref[y, tile, :, LATENT:] = grope[b, at : at + ROWS, :].astype(bf16)


def project_kernel(
    x_ref, query_ref, grad_ref, key_up_ref, value_up_ref, sgrad_ref, weights_ref, klat, krope,
    attn_ref, qgrad_ref, w0_ref, w1_ref, w2_ref, w3_ref,
    wgrad,
):
    heads = range(HEADS_STEP)
    nope = [query_ref[:, h * QDIM : h * QDIM + HEAD_DIM] for h in heads]
    grad = [grad_ref[:, h * HEAD_DIM : (h + 1) * HEAD_DIM] for h in heads]
    key_up = [key_up_ref[:, h * HEAD_DIM : (h + 1) * HEAD_DIM] for h in heads]
    value_up = [value_up_ref[:, h * HEAD_DIM : (h + 1) * HEAD_DIM] for h in heads]
    mixed_parts, full_parts, rope_parts = [], [], []
    for b in range(BLOCKS_DEV):
        score_grad = sgrad_ref[b]
        mixed_parts.append(dot(weights_ref[b], klat[b]).astype(bf16))
        full_parts.append(dot(score_grad, klat[b]).astype(bf16))
        rope_parts.append(dot(score_grad, krope[b]).astype(bf16))

    def head_rows(parts, h):
        return jnp.concatenate([part[h * BLOCK : (h + 1) * BLOCK] for part in parts], axis=0)

    width = HEADS_STEP * HEAD_DIM
    for h in heads:
        mixed = head_rows(mixed_parts, h)
        full = head_rows(full_parts, h)
        attn_ref[:, h * HEAD_DIM : (h + 1) * HEAD_DIM] = dot(mixed, value_up[h]).astype(bf16)
        qgrad_ref[:, h * QDIM : h * QDIM + HEAD_DIM] = dot(full, key_up[h]).astype(bf16)
        qgrad_ref[:, h * QDIM + HEAD_DIM : (h + 1) * QDIM] = head_rows(rope_parts, h)
        at = h * HEAD_DIM
        wgrad[:, at : at + HEAD_DIM] = dot_tn(full, nope[h]).astype(bf16)
        wgrad[:, width + at : width + at + HEAD_DIM] = dot_tn(mixed, grad[h]).astype(bf16)

    for r, out in enumerate((w0_ref, w1_ref, w2_ref, w3_ref)):
        start = pl.multiple_of(((x_ref[0] + r) % NX) * PART, PART)
        out[...] = wgrad[pl.ds(start, PART), :]


def pair_kernel(keep_ref, recv_ref, own_ref, s1_ref, s2_ref, s3_ref):
    for r, out in enumerate((own_ref, s1_ref, s2_ref, s3_ref)):
        y = (NY - r) % NY
        out[...] = (keep_ref[y] + recv_ref[y].astype(f32)).astype(out.dtype)


def slots_kernel(own_ref, r1_ref, r2_ref, r3_ref, mine_ref, out_ref):
    total = own_ref[...] + r1_ref[...].astype(f32) + r2_ref[...].astype(f32) + r3_ref[...].astype(f32)
    mine_ref[...] = total[:BLOCKS_DEV]
    out_ref[...] = total[BLOCKS_DEV:].astype(bf16)


def column_kernel(x_ref, z_ref, l0, l1, l2, l3, mine_ref, i0, i1, i2, i3, out_ref, acc):
    acc[...] = jnp.zeros_like(acc)
    for b in range(BLOCKS_DEV):
        acc[z_ref[0] * BLOCKS_DEV + b] = mine_ref[b]
    for listed, in_ref in ((l0, i0), (l1, i1), (l2, i2), (l3, i3)):
        for s in range(BLOCKS_DEV * SLOTS):
            block = listed[s]

            @pl.when(block // COLUMN == x_ref[0])
            def _():
                at = block % COLUMN
                acc[at] = acc[at] + in_ref[s].astype(f32)

    for z in range(NZ):
        for b in range(BLOCKS_DEV):
            out_ref[z, b] = acc[z * BLOCKS_DEV + b].astype(bf16)


def line_kernel(in_ref, out_ref):
    total = in_ref[0].astype(f32)
    for z in range(1, NZ):
        total = total + in_ref[z].astype(f32)
    out_ref[...] = total.astype(bf16)


def part_kernel(w0, w1, w2, w3, out_ref):
    for z in range(NZ):
        rows = slice(z * ROWS, (z + 1) * ROWS)
        out_ref[z] = sum(ref[rows].astype(f32) for ref in (w0, w1, w2, w3)).astype(bf16)


def weights_kernel(in_ref, key_ref, value_ref):
    total = sum(in_ref[z].astype(f32) for z in range(NZ))
    for h in range(HEADS_DEV):
        at = (h // HEADS_STEP) * 2 * HEADS_STEP * HEAD_DIM + (h % HEADS_STEP) * HEAD_DIM
        key_ref[:, h, :] = total[:, at : at + HEAD_DIM]
        at = at + HEADS_STEP * HEAD_DIM
        value_ref[:, h, :] = total[:, at : at + HEAD_DIM]


def cores_kernel(core_ref, near_ref, far_ref, out_ref):
    for b in range(BLOCKS_DEV):
        out_ref[b, core_ref[0]] = near_ref[b]
        out_ref[b, 1 - core_ref[0]] = far_ref[b]


def final_kernel(y_ref, i0, i1, i2, i3, latent_ref, gain_ref, out_ref):
    for r, in_ref in enumerate((i0, i1, i2, i3)):
        y = (y_ref[0] - r + NY) % NY
        for b in range(BLOCKS_DEV):
            total = in_ref[b].reshape(NC * ROWS, KV).astype(f32)
            rows = pl.ds(pl.multiple_of(b * BLOCK + y * NC * ROWS, NC * ROWS), NC * ROWS)
            raw = latent_ref[rows, :LATENT].astype(f32)
            inverse = norm_inverse(raw)
            gained = total[:, :LATENT] * gain_ref[...]
            out_ref[rows, :LATENT] = inverse * gained - raw * inverse * inverse * inverse * jnp.mean(
                raw * gained, axis=1, keepdims=True
            )
            out_ref[rows, LATENT:] = total[:, LATENT:]


def call(kernel, out_shape, in_specs, limit=VMEM_LIMIT, **kw):
    return pl.pallas_call(
        kernel,
        out_shape=out_shape,
        in_specs=in_specs,
        out_specs=kw.pop("out_specs", vmem()),
        compiler_params=pltpu.CompilerParams(vmem_limit_bytes=limit),
        **kw,
    )


def shape(*dims, dtype=bf16):
    return jax.ShapeDtypeStruct(dims, dtype)


def exchange(values, axis):
    return lax.all_to_all(values, axis, split_axis=0, concat_axis=0, tiled=True)


def shift(values, axis, count, by):
    return lax.ppermute(values, axis, [(i, (i + by) % count) for i in range(count)])


def in_hbm(values):
    return pltpu.with_memory_space_constraint(values, pltpu.HBM)


def swap_cores(values):
    return lax.ppermute(values, "c", [(0, 1), (1, 0)])


def columns(rows, cols):
    return pl.BlockSpec((rows, cols), lambda g: (0, g))


def whole(*dims):
    return pl.BlockSpec(dims, lambda g: (0,) * len(dims))


def cost(flops):
    return pl.CostEstimate(flops=flops, bytes_accessed=8_000_000, transcendentals=0)


def shards(query, latent, norm_gain, key_up, value_up, out_grad, ancestors, visible):
    def index(axis):
        return lax.axis_index(axis).astype(jnp.int32).reshape(1)

    core, x, y, z = index("c"), index("x"), index("y"), index("z")
    share = y * NC + core
    gain = norm_gain.reshape(1, LATENT)
    listed = ancestors.reshape(BLOCKS_DEV * SLOTS)
    limits = visible.reshape(BLOCKS_DEV * SLOTS)
    slots = BLOCKS_DEV * SLOTS
    lists = [listed] + [shift(listed, "x", NX, -r) for r in range(1, NX)]

    mine = call(share_kernel, shape(NZ, BLOCKS_DEV, ROWS, KV), [smem(), vmem(), vmem()])(share, latent, gain)
    key_up_flat = key_up.reshape(LATENT, HEADS_DEV * HEAD_DIM)
    value_up_flat = value_up.reshape(LATENT, HEADS_DEV * HEAD_DIM)
    column = exchange(mine, "z").reshape(COLUMN, ROWS, KV)
    column, key_up_flat, value_up_flat = lax.optimization_barrier((column, key_up_flat, value_up_flat))
    tile_list = shape(slots, ROWS, KV)
    sent = call(spread_kernel, (tile_list,) * NX, [smem()] * NX + [vmem()], out_specs=(vmem(),) * NX)(*lists, column)
    got = [sent[0]] + [shift(sent[r], "x", NX, r) for r in range(1, NX)]
    picked = call(select_kernel, tile_list, [smem()] * 2 + [vmem()] * NX)(x, listed, *got)
    near = [picked] + [shift(picked, "y", NY, r) for r in range(1, NY)]
    far = [swap_cores(piece) for piece in near]

    tokens = query.shape[0]
    steps = HEADS_DEV // HEADS_STEP
    width = HEADS_STEP * HEAD_DIM
    wcols = 2 * HEADS_DEV * HEAD_DIM
    rows = HEADS_DEV * BLOCK
    lat_keys, rope_keys = (BLOCKS_DEV, KEYS, LATENT), (BLOCKS_DEV, KEYS, ROPE)
    tiles = (NY, TILES, ROWS, KV)
    query, out_grad = in_hbm(query), in_hbm(out_grad)
    operands = (query, out_grad, key_up_flat, value_up_flat)
    operand_specs = [columns(tokens, HEADS_STEP * QDIM), columns(tokens, width), columns(LATENT, width), columns(LATENT, width)]
    by_rows = pl.BlockSpec((BLOCKS_DEV, HEADS_STEP * BLOCK, KEYS), lambda g: (0, g, 0))
    score_grad, weights, klat, krope, keep, send = call(
        attend_kernel,
        (pltpu.HBM((BLOCKS_DEV, rows, KEYS), bf16),) * 2
        + (pltpu.HBM(lat_keys, bf16), pltpu.HBM(rope_keys, bf16), pltpu.VMEM(tiles, f32), pltpu.HBM(tiles, bf16)),
        [smem()] * 3 + operand_specs + [whole(tokens, KV), whole(1, LATENT)] + [whole(slots, ROWS, KV)] * (2 * NY),
        out_specs=(by_rows, by_rows, whole(*lat_keys), whole(*rope_keys), whole(*tiles), whole(*tiles)),
        grid=(steps,),
        scratch_shapes=[
            pltpu.VMEM((BLOCKS_DEV, BLOCK, KEYS), f32),
            pltpu.VMEM(lat_keys, f32),
            pltpu.VMEM(rope_keys, f32),
            pltpu.VMEM((tokens, LATENT), bf16),
        ],
        cost_estimate=cost(6_200_000_000),
        limit=44 * 1024 * 1024,
    )(core, y, limits, *operands, latent, gain, *near, *far)

    own, s1, s2, s3 = call(
        pair_kernel,
        (shape(TILES, ROWS, KV, dtype=f32),) + (shape(TILES, ROWS, KV),) * 3,
        [vmem(), vmem()],
        out_specs=(vmem(),) * 4,
    )(keep, swap_cores(send))
    others = [shift(s, "y", NY, r) for r, s in ((1, s1), (2, s2), (3, s3))]
    own, score_grad = lax.optimization_barrier((own, score_grad))
    attn_out, query_grad, *wgrads = call(
        project_kernel,
        (shape(tokens, HEADS_DEV * HEAD_DIM), shape(tokens, HEADS_DEV * QDIM)) + (shape(PART, wcols),) * NX,
        [smem()] + operand_specs + [by_rows, by_rows, whole(*lat_keys), whole(*rope_keys)],
        out_specs=(columns(tokens, width), columns(tokens, HEADS_STEP * QDIM)) + (columns(PART, 2 * width),) * NX,
        grid=(steps,),
        scratch_shapes=[pltpu.VMEM((LATENT, 2 * width), bf16)],
        cost_estimate=cost(4_000_000_000),
    )(x, *operands, in_hbm(score_grad), in_hbm(weights), in_hbm(klat), in_hbm(krope))
    parts = [shift(w, "x", NX, r) for r, w in enumerate(wgrads) if r > 0]
    *others, wgrads[0] = lax.optimization_barrier((*others, wgrads[0]))
    own, spread = call(
        slots_kernel,
        (shape(BLOCKS_DEV, ROWS, KV, dtype=f32), shape(slots, ROWS, KV)),
        [vmem()] * 4,
        out_specs=(vmem(), vmem()),
    )(own, *others)
    others = [shift(spread, "x", NX, -r) for r in range(1, NX)]
    line = call(
        column_kernel,
        shape(NZ, BLOCKS_DEV, ROWS, KV),
        [smem()] * 6 + [vmem()] * 5,
        scratch_shapes=[pltpu.VMEM((COLUMN, ROWS, KV), f32)],
    )(x, z, *lists, own, spread, *others)
    line = exchange(line, "z")
    part = call(part_kernel, shape(NZ, ROWS, wcols), [vmem()] * NX)(wgrads[0], *parts)
    part = exchange(part, "z")
    total = call(line_kernel, shape(BLOCKS_DEV, ROWS, KV), [vmem()])(line)
    total = call(cores_kernel, shape(BLOCKS_DEV, NC, ROWS, KV), [smem(), vmem(), vmem()])(
        core, total, swap_cores(total)
    )
    others = [shift(total, "y", NY, r) for r in range(1, NY)]
    latent_grad = call(final_kernel, shape(tokens, KV, dtype=f32), [smem()] + [vmem()] * 6)(
        y, total, *others, latent, gain
    )
    grad_shape = shape(PART // NZ, HEADS_DEV, HEAD_DIM, dtype=f32)
    key_up_grad, value_up_grad = call(
        weights_kernel, (grad_shape, grad_shape), [vmem()], out_specs=(vmem(), vmem())
    )(part)
    return attn_out, query_grad, latent_grad, key_up_grad, value_up_grad


def solution(mesh):
    grid = Mesh(mesh.devices.reshape(NX, NZ, NY, NC), ("x", "z", "y", "c"))
    pos, head = ("x", "z"), ("y", "c")
    return jax.shard_map(
        shards,
        mesh=grid,
        in_specs=(
            P(pos, head),
            P(pos, None),
            P(),
            P(None, head, None),
            P(None, head, None),
            P(pos, head),
            P(pos, None),
            P(pos, None),
        ),
        out_specs=(
            P(pos, head),
            P(pos, head),
            P(pos, None),
            P(pos, head, None),
            P(pos, head, None),
        ),
        check_vma=False,
    )
```

```python
import functools
import math

import jax
import jax.numpy as jnp
from jax import lax
from jax.experimental import pallas as pl
from jax.experimental.pallas import tpu as pltpu
from jax.sharding import Mesh
from jax.sharding import PartitionSpec as P

LATENT = 512
ROPE = 64
KV = LATENT + ROPE
HEAD_DIM = 128
QDIM = HEAD_DIM + ROPE
BLOCK = 128
SLOTS = 4
BLOCKS_DEV = 2
NX, NZ, NY, NC = 4, 8, 4, 2
SHARES = NY * NC
ROWS = BLOCK // SHARES
HALF = NY * ROWS
HEADS_DEV = 8
TILES = BLOCKS_DEV * (1 + SLOTS)
KEYS = (1 + SLOTS) * BLOCK
COLUMN = NZ * BLOCKS_DEV
PART = LATENT // NX
HEADS_STEP = 4
norm_epsilon = 1e-06

bf16 = jnp.bfloat16
f32 = jnp.float32
VMEM_LIMIT = 48 * 1024 * 1024


def dot(a, b):
    return lax.dot_general(a, b, (((1,), (0,)), ((), ())), preferred_element_type=f32)


def dot_nt(a, b):
    return lax.dot_general(a, b, (((1,), (1,)), ((), ())), preferred_element_type=f32)


def dot_tn(a, b):
    return lax.dot_general(a, b, (((0,), (0,)), ((), ())), preferred_element_type=f32)


def smem():
    return pl.BlockSpec(memory_space=pltpu.SMEM)


def vmem():
    return pl.BlockSpec(memory_space=pltpu.VMEM)


def norm_inverse(raw):
    return lax.rsqrt(jnp.mean(raw * raw, axis=1, keepdims=True) + norm_epsilon)


def share_kernel(share_ref, latent_ref, gain_ref, out_ref):
    for b in range(BLOCKS_DEV):
        start = pl.multiple_of(b * BLOCK + share_ref[0] * ROWS, ROWS)
        raw = latent_ref[pl.ds(start, ROWS), :LATENT].astype(f32)
        keys = (raw * norm_inverse(raw) * gain_ref[...]).astype(bf16)
        rope = latent_ref[pl.ds(start, ROWS), LATENT:]
        for z in range(NZ):
            out_ref[z, b, :, :LATENT] = keys
            out_ref[z, b, :, LATENT:] = rope


def spread_kernel(l0, l1, l2, l3, column_ref, o0, o1, o2, o3):
    for listed, out in ((l0, o0), (l1, o1), (l2, o2), (l3, o3)):
        for s in range(BLOCKS_DEV * SLOTS):
            out[s] = column_ref[listed[s] % COLUMN]


def select_kernel(x_ref, listed_ref, i0, i1, i2, i3, out_ref):
    for s in range(BLOCKS_DEV * SLOTS):
        back = (x_ref[0] - listed_ref[s] // COLUMN + NX) % NX
        for r, in_ref in enumerate((i0, i1, i2, i3)):

            @pl.when(back == r)
            def _():
                out_ref[s] = in_ref[s]


def attend_kernel(
    core_ref, y_ref, vis_ref, query_ref, grad_ref, key_up_ref, value_up_ref, latent_ref, gain_ref,
    n0, n1, n2, n3, f0, f1, f2, f3,
    sgrad_ref, weights_ref, klat, krope, keep_ref, send_ref,
    bias, glat, grope, own,
):
    step = pl.program_id(0)
    core = core_ref[0]
    scale = 1.0 / math.sqrt(QDIM)

    @pl.when(step == 0)
    def _():
        raw = latent_ref[:, :LATENT].astype(f32)
        own[...] = (raw * norm_inverse(raw) * gain_ref[...]).astype(bf16)
        for side, pieces in enumerate(((n0, n1, n2, n3), (f0, f1, f2, f3))):
            for r, piece in enumerate(pieces):
                at = side * HALF + r * ROWS
                owner = (y_ref[0] - r + NY) % NY * NC + (core + side) % NC
                for b in range(BLOCKS_DEV):
                    rows = pl.ds(pl.multiple_of(b * BLOCK + owner * ROWS, ROWS), ROWS)
                    klat[b, at : at + ROWS, :] = own[rows, :]
                    krope[b, at : at + ROWS, :] = latent_ref[rows, LATENT:]
                    for j in range(SLOTS):
                        to = (1 + j) * BLOCK + at
                        klat[b, to : to + ROWS, :] = piece[b * SLOTS + j, :, :LATENT]
                        krope[b, to : to + ROWS, :] = piece[b * SLOTS + j, :, LATENT:]
        col = lax.broadcasted_iota(jnp.int32, (BLOCK, BLOCK), 1)
        row = lax.broadcasted_iota(jnp.int32, (BLOCK, BLOCK), 0)
        side = jnp.where(col >= HALF, 1, 0)
        rest = col - side * HALF
        piece = (y_ref[0] - rest // ROWS + NY) % NY
        owner = jnp.where(core == 0, side, 1 - side)
        offset = (piece * NC + owner) * ROWS + rest % ROWS
        for b in range(BLOCKS_DEV):
            bias[b, :, :BLOCK] = jnp.where(offset <= row, 0.0, -jnp.inf)
            for j in range(SLOTS):
                limit = vis_ref[b * SLOTS + j]
                bias[b, :, (1 + j) * BLOCK : (2 + j) * BLOCK] = jnp.where(offset < limit, 0.0, -jnp.inf)
        glat[...] = jnp.zeros_like(glat)
        grope[...] = jnp.zeros_like(grope)

    heads = range(HEADS_STEP)
    nope = [query_ref[:, h * QDIM : h * QDIM + HEAD_DIM] for h in heads]
    rope = [query_ref[:, h * QDIM + HEAD_DIM : (h + 1) * QDIM] for h in heads]
    grad = [grad_ref[:, h * HEAD_DIM : (h + 1) * HEAD_DIM] for h in heads]
    key_up = [key_up_ref[:, h * HEAD_DIM : (h + 1) * HEAD_DIM] for h in heads]
    value_up = [value_up_ref[:, h * HEAD_DIM : (h + 1) * HEAD_DIM] for h in heads]
    absorbed = [dot_nt(nope[h], key_up[h]).astype(bf16) for h in heads]
    mixed_grad = [dot_nt(grad[h], value_up[h]).astype(bf16) for h in heads]

    staged = []
    for b in range(BLOCKS_DEV):
        rows = slice(b * BLOCK, (b + 1) * BLOCK)
        ab = jnp.concatenate([absorbed[h][rows] for h in heads], axis=0)
        rb = jnp.concatenate([rope[h][rows] for h in heads], axis=0)
        mg = jnp.concatenate([mixed_grad[h][rows] for h in heads], axis=0)
        scores = dot_nt(ab, klat[b]) + dot_nt(rb, krope[b])
        staged.append((ab, rb, mg, scores, dot_nt(mg, klat[b])))
    for b, (ab, rb, mg, scores, weight_grad) in enumerate(staged):
        mask = jnp.concatenate([bias[b]] * HEADS_STEP, axis=0)
        scores = scores * (scale * math.log2(math.e)) + mask
        exp_terms = jnp.exp2(scores - jnp.max(scores, axis=1, keepdims=True))
        weights = exp_terms * (1.0 / jnp.sum(exp_terms, axis=1, keepdims=True))
        half = weights.astype(bf16)
        weights_ref[b] = half
        inner = jnp.sum(weights * weight_grad, axis=1, keepdims=True)
        score_grad = (weights * (weight_grad - inner) * scale).astype(bf16)
        sgrad_ref[b] = score_grad
        both = jnp.concatenate([score_grad, half], axis=0)
        glat[b] += dot_tn(both, jnp.concatenate([ab, mg], axis=0))
        grope[b] += dot_tn(score_grad, rb)

    @pl.when(step == pl.num_programs(0) - 1)
    def _():
        for b in range(BLOCKS_DEV):
            for j in range(1 + SLOTS):
                tile = b if j == 0 else BLOCKS_DEV + b * SLOTS + j - 1
                for y in range(NY):
                    at = j * BLOCK + y * ROWS
                    keep_ref[y, tile, :, :LATENT] = glat[b, at : at + ROWS, :]
                    keep_ref[y, tile, :, LATENT:] = grope[b, at : at + ROWS, :]
                    at = at + HALF
                    send_ref[y, tile, :, :LATENT] = glat[b, at : at + ROWS, :].astype(bf16)
                    send_ref[y, tile, :, LATENT:] = grope[b, at : at + ROWS, :].astype(bf16)


def project_kernel(
    x_ref, query_ref, grad_ref, key_up_ref, value_up_ref, sgrad_ref, weights_ref, klat, krope,
    attn_ref, qgrad_ref, w0_ref, w1_ref, w3_ref, w2a_ref, w2b_ref,
    wgrad,
):
    heads = range(HEADS_STEP)
    nope = [query_ref[:, h * QDIM : h * QDIM + HEAD_DIM] for h in heads]
    grad = [grad_ref[:, h * HEAD_DIM : (h + 1) * HEAD_DIM] for h in heads]
    key_up = [key_up_ref[:, h * HEAD_DIM : (h + 1) * HEAD_DIM] for h in heads]
    value_up = [value_up_ref[:, h * HEAD_DIM : (h + 1) * HEAD_DIM] for h in heads]
    mixed_parts, full_parts, rope_parts = [], [], []
    for b in range(BLOCKS_DEV):
        score_grad = sgrad_ref[b]
        mixed_parts.append(dot(weights_ref[b], klat[b]).astype(bf16))
        full_parts.append(dot(score_grad, klat[b]).astype(bf16))
        rope_parts.append(dot(score_grad, krope[b]).astype(bf16))

    def head_rows(parts, h):
        return jnp.concatenate([part[h * BLOCK : (h + 1) * BLOCK] for part in parts], axis=0)

    width = HEADS_STEP * HEAD_DIM
    for h in heads:
        mixed = head_rows(mixed_parts, h)
        full = head_rows(full_parts, h)
        attn_ref[:, h * HEAD_DIM : (h + 1) * HEAD_DIM] = dot(mixed, value_up[h]).astype(bf16)
        qgrad_ref[:, h * QDIM : h * QDIM + HEAD_DIM] = dot(full, key_up[h]).astype(bf16)
        qgrad_ref[:, h * QDIM + HEAD_DIM : (h + 1) * QDIM] = head_rows(rope_parts, h)
        at = h * HEAD_DIM
        wgrad[:, at : at + HEAD_DIM] = dot_tn(full, nope[h]).astype(bf16)
        wgrad[:, width + at : width + at + HEAD_DIM] = dot_tn(mixed, grad[h]).astype(bf16)

    for out, r, skip in ((w0_ref, 0, 0), (w1_ref, 1, 0), (w3_ref, 3, 0), (w2a_ref, 2, 0), (w2b_ref, 2, PART // 2)):
        start = pl.multiple_of(((x_ref[0] + r) % NX) * PART + skip, PART // 2)
        out[...] = wgrad[pl.ds(start, out.shape[0]), :]


def relay_kernel(w1_ref, w3_ref, a_ref, b_ref, u1_ref, u3_ref):
    half = PART // 2
    u1_ref[:half] = (w1_ref[:half].astype(f32) + a_ref[...].astype(f32)).astype(bf16)
    u1_ref[half:] = w1_ref[half:]
    u3_ref[:half] = w3_ref[:half]
    u3_ref[half:] = (w3_ref[half:].astype(f32) + b_ref[...].astype(f32)).astype(bf16)


def pair_kernel(keep_ref, recv_ref, own_ref, s1_ref, s2_ref, s3_ref):
    for r, out in enumerate((own_ref, s1_ref, s2_ref, s3_ref)):
        y = (NY - r) % NY
        out[...] = (keep_ref[y] + recv_ref[y].astype(f32)).astype(out.dtype)


def slots_kernel(own_ref, r1_ref, r2_ref, r3_ref, mine_ref, out_ref):
    total = own_ref[...] + r1_ref[...].astype(f32) + r2_ref[...].astype(f32) + r3_ref[...].astype(f32)
    mine_ref[...] = total[:BLOCKS_DEV]
    out_ref[...] = total[BLOCKS_DEV:].astype(bf16)


def column_kernel(x_ref, z_ref, l0, l1, l2, l3, mine_ref, i0, i1, i2, i3, out_ref, acc):
    acc[...] = jnp.zeros_like(acc)
    for b in range(BLOCKS_DEV):
        acc[z_ref[0] * BLOCKS_DEV + b] = mine_ref[b]
    for listed, in_ref in ((l0, i0), (l1, i1), (l2, i2), (l3, i3)):
        for s in range(BLOCKS_DEV * SLOTS):
            block = listed[s]

            @pl.when(block // COLUMN == x_ref[0])
            def _():
                at = block % COLUMN
                acc[at] = acc[at] + in_ref[s].astype(f32)

    for z in range(NZ):
        for b in range(BLOCKS_DEV):
            out_ref[z, b] = acc[z * BLOCKS_DEV + b].astype(bf16)


def line_kernel(in_ref, out_ref):
    total = in_ref[0].astype(f32)
    for z in range(1, NZ):
        total = total + in_ref[z].astype(f32)
    out_ref[...] = total.astype(bf16)


def part_kernel(w0, w1, w3, out_ref):
    for z in range(NZ):
        rows = slice(z * ROWS, (z + 1) * ROWS)
        out_ref[z] = sum(ref[rows].astype(f32) for ref in (w0, w1, w3)).astype(bf16)


def weights_kernel(in_ref, key_ref, value_ref):
    total = sum(in_ref[z].astype(f32) for z in range(NZ))
    for h in range(HEADS_DEV):
        at = (h // HEADS_STEP) * 2 * HEADS_STEP * HEAD_DIM + (h % HEADS_STEP) * HEAD_DIM
        key_ref[:, h, :] = total[:, at : at + HEAD_DIM]
        at = at + HEADS_STEP * HEAD_DIM
        value_ref[:, h, :] = total[:, at : at + HEAD_DIM]


def cores_kernel(core_ref, near_ref, far_ref, out_ref):
    for b in range(BLOCKS_DEV):
        out_ref[b, core_ref[0]] = near_ref[b]
        out_ref[b, 1 - core_ref[0]] = far_ref[b]


def final_kernel(y_ref, i0, i1, i2, i3, latent_ref, gain_ref, out_ref):
    for r, in_ref in enumerate((i0, i1, i2, i3)):
        y = (y_ref[0] - r + NY) % NY
        for b in range(BLOCKS_DEV):
            total = in_ref[b].reshape(NC * ROWS, KV).astype(f32)
            rows = pl.ds(pl.multiple_of(b * BLOCK + y * NC * ROWS, NC * ROWS), NC * ROWS)
            raw = latent_ref[rows, :LATENT].astype(f32)
            inverse = norm_inverse(raw)
            gained = total[:, :LATENT] * gain_ref[...]
            out_ref[rows, :LATENT] = inverse * gained - raw * inverse * inverse * inverse * jnp.mean(
                raw * gained, axis=1, keepdims=True
            )
            out_ref[rows, LATENT:] = total[:, LATENT:]


def call(kernel, out_shape, in_specs, limit=VMEM_LIMIT, **kw):
    return pl.pallas_call(
        kernel,
        out_shape=out_shape,
        in_specs=in_specs,
        out_specs=kw.pop("out_specs", vmem()),
        compiler_params=pltpu.CompilerParams(vmem_limit_bytes=limit),
        **kw,
    )


def shape(*dims, dtype=bf16):
    return jax.ShapeDtypeStruct(dims, dtype)


def exchange(values, axis):
    return lax.all_to_all(values, axis, split_axis=0, concat_axis=0, tiled=True)


def shift(values, axis, count, by):
    return lax.ppermute(values, axis, [(i, (i + by) % count) for i in range(count)])


def in_hbm(values):
    return pltpu.with_memory_space_constraint(values, pltpu.HBM)


def swap_cores(values):
    return lax.ppermute(values, "c", [(0, 1), (1, 0)])


def columns(rows, cols):
    return pl.BlockSpec((rows, cols), lambda g: (0, g))


def whole(*dims):
    return pl.BlockSpec(dims, lambda g: (0,) * len(dims))


def cost(flops):
    return pl.CostEstimate(flops=flops, bytes_accessed=8_000_000, transcendentals=0)


def shards(query, latent, norm_gain, key_up, value_up, out_grad, ancestors, visible):
    def index(axis):
        return lax.axis_index(axis).astype(jnp.int32).reshape(1)

    core, x, y, z = index("c"), index("x"), index("y"), index("z")
    share = y * NC + core
    gain = norm_gain.reshape(1, LATENT)
    listed = ancestors.reshape(BLOCKS_DEV * SLOTS)
    limits = visible.reshape(BLOCKS_DEV * SLOTS)
    slots = BLOCKS_DEV * SLOTS
    lists = [listed] + [shift(listed, "x", NX, -r) for r in range(1, NX)]

    mine = call(share_kernel, shape(NZ, BLOCKS_DEV, ROWS, KV), [smem(), vmem(), vmem()])(share, latent, gain)
    key_up_flat = key_up.reshape(LATENT, HEADS_DEV * HEAD_DIM)
    value_up_flat = value_up.reshape(LATENT, HEADS_DEV * HEAD_DIM)
    column = exchange(mine, "z").reshape(COLUMN, ROWS, KV)
    column, key_up_flat, value_up_flat = lax.optimization_barrier((column, key_up_flat, value_up_flat))
    tile_list = shape(slots, ROWS, KV)
    sent = call(spread_kernel, (tile_list,) * NX, [smem()] * NX + [vmem()], out_specs=(vmem(),) * NX)(*lists, column)
    got = [sent[0]] + [shift(sent[r], "x", NX, r) for r in range(1, NX)]
    picked = call(select_kernel, tile_list, [smem()] * 2 + [vmem()] * NX)(x, listed, *got)
    near = [picked] + [shift(picked, "y", NY, r) for r in range(1, NY)]
    far = [swap_cores(piece) for piece in near]

    tokens = query.shape[0]
    steps = HEADS_DEV // HEADS_STEP
    width = HEADS_STEP * HEAD_DIM
    wcols = 2 * HEADS_DEV * HEAD_DIM
    rows = HEADS_DEV * BLOCK
    lat_keys, rope_keys = (BLOCKS_DEV, KEYS, LATENT), (BLOCKS_DEV, KEYS, ROPE)
    tiles = (NY, TILES, ROWS, KV)
    query, out_grad = in_hbm(query), in_hbm(out_grad)
    operands = (query, out_grad, key_up_flat, value_up_flat)
    operand_specs = [columns(tokens, HEADS_STEP * QDIM), columns(tokens, width), columns(LATENT, width), columns(LATENT, width)]
    by_rows = pl.BlockSpec((BLOCKS_DEV, HEADS_STEP * BLOCK, KEYS), lambda g: (0, g, 0))
    score_grad, weights, klat, krope, keep, send = call(
        attend_kernel,
        (pltpu.HBM((BLOCKS_DEV, rows, KEYS), bf16),) * 2
        + (pltpu.HBM(lat_keys, bf16), pltpu.HBM(rope_keys, bf16), pltpu.VMEM(tiles, f32), pltpu.HBM(tiles, bf16)),
        [smem()] * 3 + operand_specs + [whole(tokens, KV), whole(1, LATENT)] + [whole(slots, ROWS, KV)] * (2 * NY),
        out_specs=(by_rows, by_rows, whole(*lat_keys), whole(*rope_keys), whole(*tiles), whole(*tiles)),
        grid=(steps,),
        scratch_shapes=[
            pltpu.VMEM((BLOCKS_DEV, BLOCK, KEYS), f32),
            pltpu.VMEM(lat_keys, f32),
            pltpu.VMEM(rope_keys, f32),
            pltpu.VMEM((tokens, LATENT), bf16),
        ],
        cost_estimate=cost(6_200_000_000),
        limit=44 * 1024 * 1024,
    )(core, y, limits, *operands, latent, gain, *near, *far)

    own, s1, s2, s3 = call(
        pair_kernel,
        (shape(TILES, ROWS, KV, dtype=f32),) + (shape(TILES, ROWS, KV),) * 3,
        [vmem(), vmem()],
        out_specs=(vmem(),) * 4,
    )(keep, swap_cores(send))
    others = [shift(s, "y", NY, r) for r, s in ((1, s1), (2, s2), (3, s3))]
    own, score_grad = lax.optimization_barrier((own, score_grad))
    attn_out, query_grad, *wgrads = call(
        project_kernel,
        (shape(tokens, HEADS_DEV * HEAD_DIM), shape(tokens, HEADS_DEV * QDIM)) + (shape(PART, wcols),) * 3 + (shape(PART // 2, wcols),) * 2,
        [smem()] + operand_specs + [by_rows, by_rows, whole(*lat_keys), whole(*rope_keys)],
        out_specs=(columns(tokens, width), columns(tokens, HEADS_STEP * QDIM)) + (columns(PART, 2 * width),) * 3 + (columns(PART // 2, 2 * width),) * 2,
        grid=(steps,),
        scratch_shapes=[pltpu.VMEM((LATENT, 2 * width), bf16)],
        cost_estimate=cost(4_000_000_000),
    )(x, *operands, in_hbm(score_grad), in_hbm(weights), in_hbm(klat), in_hbm(krope))
    w0, w1, w3, w2a, w2b = wgrads
    relayed = (shift(w2a, "x", NX, 1), shift(w2b, "x", NX, -1))
    u1, u3 = call(relay_kernel, (shape(PART, wcols),) * 2, [vmem()] * 4, out_specs=(vmem(),) * 2)(w1, w3, *relayed)
    parts = [shift(u1, "x", NX, 1), shift(u3, "x", NX, -1)]
    *others, w0 = lax.optimization_barrier((*others, w0))
    own, spread = call(
        slots_kernel,
        (shape(BLOCKS_DEV, ROWS, KV, dtype=f32), shape(slots, ROWS, KV)),
        [vmem()] * 4,
        out_specs=(vmem(), vmem()),
    )(own, *others)
    others = [shift(spread, "x", NX, -r) for r in range(1, NX)]
    line = call(
        column_kernel,
        shape(NZ, BLOCKS_DEV, ROWS, KV),
        [smem()] * 6 + [vmem()] * 5,
        scratch_shapes=[pltpu.VMEM((COLUMN, ROWS, KV), f32)],
    )(x, z, *lists, own, spread, *others)
    line = exchange(line, "z")
    part = call(part_kernel, shape(NZ, ROWS, wcols), [vmem()] * 3)(w0, *parts)
    part = exchange(part, "z")
    total = call(line_kernel, shape(BLOCKS_DEV, ROWS, KV), [vmem()])(line)
    total = call(cores_kernel, shape(BLOCKS_DEV, NC, ROWS, KV), [smem(), vmem(), vmem()])(
        core, total, swap_cores(total)
    )
    others = [shift(total, "y", NY, r) for r in range(1, NY)]
    latent_grad = call(final_kernel, shape(tokens, KV, dtype=f32), [smem()] + [vmem()] * 6)(
        y, total, *others, latent, gain
    )
    grad_shape = shape(PART // NZ, HEADS_DEV, HEAD_DIM, dtype=f32)
    key_up_grad, value_up_grad = call(
        weights_kernel, (grad_shape, grad_shape), [vmem()], out_specs=(vmem(), vmem())
    )(part)
    return attn_out, query_grad, latent_grad, key_up_grad, value_up_grad


def solution(mesh):
    grid = Mesh(mesh.devices.reshape(NX, NZ, NY, NC), ("x", "z", "y", "c"))
    pos, head = ("x", "z"), ("y", "c")
    return jax.shard_map(
        shards,
        mesh=grid,
        in_specs=(
            P(pos, head),
            P(pos, None),
            P(),
            P(None, head, None),
            P(None, head, None),
            P(pos, head),
            P(pos, None),
            P(pos, None),
        ),
        out_specs=(
            P(pos, head),
            P(pos, head),
            P(pos, None),
            P(pos, head, None),
            P(pos, head, None),
        ),
        check_vma=False,
    )
```
